512 devices in a mesh: chan: 8 (over z_lo), base: 64 (over z_hi, x, y, core).
Axes of the slice: x: 4, y: 4, z: 16 (z_hi: 2, z_lo: 8; z = z_hi * 8 + z_lo), core: 2. Of those that a mesh axis runs over, the one named last changes fastest.
Arguments:
- screens: bfloat16 [256, 8, 4096], P('base'), may hold values from -6 to 6
- direction: bfloat16 [256, 8, 4096], P('base'), may hold values from -6 to 6
- sky: bfloat16 [16, 64, 1024], P(None, 'chan'), may hold values from 0.25 to 2
- weights: bfloat16 [2048, 64, 1024], P('base', 'chan'), may hold values from 0.049804688 to 1
- pairs: int32 [2048, 2], P('base'), may hold values from 0 to 255, as said below
- pointing: int32 [2048], P('base'), may hold values from 0 to 15
- counts: int32 [64], P('base'), may hold values from 8 to 32, as said below
Outputs:
- product: float32 [256, 8, 4096], P('base')
The draws below stay inside these ranges and needn't reach their ends.
Inputs may be any that keep to these rules, and one draw needn't show every extreme that they name: `pairs`: station s is owned by base index s // 4. Both stations of a slot on base index b are owned by base indices within 2 of b, counting cyclically; the two stations of a slot differ. `counts`: some base index has all its slots live in every draw; the live slots of a base index are its first ones.
All inputs are finite; a program needn't handle non-finite values.
Results may differ from the reference program's by a relative error of at most 0.0043.
Values may be sent and summed in bfloat16 or wider, within the bound.
No kernel may reach another device: no remote copies, remote signals or barrier semaphores. Data moves between devices by JAX's collectives and lax.ppermute only.
A program may use at most 64 MiB of HBM per device.

```python
import math
import jax
import jax.numpy as jnp
from jax import lax

G = 64
W = 32
PTS = 16
REACH = 2
ST_DEV = 4
SUB_DEV = 32
STATIONS = 256
SUBGRIDS = 2048
CHANNELS = 64


def draw_pairs(key, part):
    key = jax.random.fold_in(key, 11)
    owners_total = SUBGRIDS // SUB_DEV
    key_a, key_b, key_c, key_d = jax.random.split(key, 4)
    home_base = jnp.arange(SUBGRIDS, dtype=jnp.int32) // SUB_DEV
    shift_p = jax.random.randint(key_a, (SUBGRIDS,), -REACH, REACH + 1)
    shift_q = jax.random.randint(key_b, (SUBGRIDS,), -REACH, REACH + 1)
    member_p = jax.random.randint(key_c, (SUBGRIDS,), 0, ST_DEV)
    member_q = jax.random.randint(key_d, (SUBGRIDS,), 0, ST_DEV)
    clash = (shift_p == shift_q) & (member_p == member_q)
    moved = jnp.where(shift_q == REACH, shift_q - 1, shift_q + 1)
    shift_q = jnp.where(clash, moved, shift_q)
    owner_p = (home_base + shift_p) % owners_total
    owner_q = (home_base + shift_q) % owners_total
    station_p = owner_p * ST_DEV + member_p
    station_q = owner_q * ST_DEV + member_q
    return jnp.stack([station_p, station_q], axis=1).astype(jnp.int32)


def draw_counts(key, part):
    key = jax.random.fold_in(key, 23)
    owners_total = SUBGRIDS // SUB_DEV
    key_a, key_b = jax.random.split(key, 2)
    drawn = jax.random.randint(key_a, (owners_total,), SUB_DEV // 4, SUB_DEV + 1)
    busiest = jax.random.randint(key_b, (), 0, owners_total)
    filled = jnp.where(jnp.arange(owners_total, dtype=jnp.int32) == busiest, SUB_DEV, drawn)
    return filled.astype(jnp.int32)


def with_ends(result, rng, least, largest):
    spot = [jax.random.randint(jax.random.fold_in(rng, axis), (), 0, length) for axis, length in enumerate(result.shape)]
    widest = result.shape.index(max(result.shape))
    beside = spot[:widest] + [(spot[widest] + 1) % result.shape[widest]] + spot[widest + 1:]
    return result.at[tuple(spot)].set(least).at[tuple(beside)].set(largest)


def level_of(key, shape, pieces, least, top_value):
    gain, own = 1.0, jax.random.fold_in(key, 6)
    for dim, blocks in pieces:
        heights = jnp.exp(jax.random.uniform(jax.random.fold_in(own, dim), (blocks,), jnp.float32, least / len(pieces), top_value / len(pieces)))
        gain = gain * jnp.repeat(heights, shape[dim] // blocks).reshape([-1 if axis == dim else 1 for axis in range(len(shape))])
    return gain


def gaussian(stream_key, shape, scale, limit, cuts=(), kind=jnp.bfloat16):
    array = scale * jax.random.normal(stream_key, shape, jnp.float32)
    if cuts:
        array = array * level_of(stream_key, shape, cuts, -0.22, 0.18)
    return jnp.clip(array, -limit, limit).astype(kind)


def setup_inputs(seed: int = 0) -> dict:
    splits = jax.random.split(jax.random.key(seed), 8)
    screens = gaussian(splits[0], (STATIONS, 8, G * G), 1.0, 6.0, ((0, 64),))
    direction = gaussian(splits[1], (STATIONS, 8, G * G), 1.0, 6.0, ((0, 64),))
    sky = jnp.clip(jnp.exp(math.log(2.0) - 2.0794415 * jax.random.uniform(splits[2], (PTS, CHANNELS, W * W), jnp.float32) ** level_of(splits[2], (PTS, CHANNELS, W * W), ((1, 8),), -0.2, 0.2)), 0.25, 2.0).astype(jnp.bfloat16)
    weights = jnp.clip(jnp.exp(math.log(1.0) - 2.9996462 * jax.random.uniform(splits[3], (SUBGRIDS, CHANNELS, W * W), jnp.float32) ** level_of(splits[3], (SUBGRIDS, CHANNELS, W * W), ((0, 64), (1, 8)), -0.2, 0.2)), 0.049804688, 1.0).astype(jnp.bfloat16)
    pairs = draw_pairs(jax.random.fold_in(splits[7], 71), 0)
    pointing = with_ends(jax.random.randint(splits[5], (SUBGRIDS,), 0, PTS), jax.random.fold_in(splits[5], 1), 0, PTS - 1).astype(jnp.int32)
    counts = draw_counts(jax.random.fold_in(splits[7], 71), 0)
    return {"screens": screens, "direction": direction, "sky": sky, "weights": weights, "pairs": pairs, "pointing": pointing, "counts": counts}


def to_half(values):
    return lax.optimization_barrier(values.astype(jnp.bfloat16)).astype(jnp.float32)

def dft_tables(length):
    position = jnp.arange(length, dtype=jnp.int32)
    product = position[:, None] * position[None, :] % length
    angles = product.astype(jnp.float32) * (2.0 * math.pi / length)
    norm_factor = 1.0 / math.sqrt(length)
    return (to_half(jnp.cos(angles) * norm_factor), to_half(jnp.sin(angles) * norm_factor))

def transform(real_in, imag_in, cosine_table, sine_table, inverse):
    sine_signed = sine_table if inverse else -sine_table
    highest = lax.Precision.HIGHEST

    def along_axis(pattern, part_real, part_imag):
        out_real = jnp.einsum(pattern, part_real, cosine_table, precision=highest) - jnp.einsum(pattern, part_imag, sine_signed, precision=highest)
        out_imag = jnp.einsum(pattern, part_real, sine_signed, precision=highest) + jnp.einsum(pattern, part_imag, cosine_table, precision=highest)
        return (out_real, out_imag)
    mid_real, mid_imag = along_axis('...rc,cd->...rd', real_in, imag_in)
    return along_axis('...rd,re->...ed', to_half(mid_real), to_half(mid_imag))

def reference(screens, direction, sky, weights, pairs, pointing, counts):
    screen_all = screens.astype(jnp.float32).reshape(STATIONS, 8, G, G)
    probe_all = direction.astype(jnp.float32).reshape(STATIONS, 8, G, G)
    screen_cplx = screen_all[:, :4] + 1j * screen_all[:, 4:]
    probe_cplx = probe_all[:, :4] + 1j * probe_all[:, 4:]
    sky_all = sky.astype(jnp.float32).reshape(PTS, CHANNELS, 1, W, W)
    cosine_table, sine_table = dft_tables(W)
    margin = G - W
    zero_index = jnp.zeros((), jnp.int32)

    def visit(totals, slot):
        out_real, out_imag = totals
        station_p = pairs[slot, 0]
        station_q = pairs[slot, 1]
        aimed = pointing[slot]
        alive = (slot % SUB_DEV < counts[slot // SUB_DEV]).astype(jnp.float32)
        row_start = (aimed // 4 * margin // 3).astype(jnp.int32)
        col_start = (aimed % 4 * margin // 3).astype(jnp.int32)

        def window(field):
            return lax.dynamic_slice(field, (zero_index, row_start, col_start), (4, W, W))
        beam_p = window(screen_cplx[station_p])
        beam_q = window(screen_cplx[station_q])
        probe_p = window(probe_cplx[station_p])
        probe_q = window(probe_cplx[station_q])
        delta = probe_p * jnp.conj(beam_q) + beam_p * jnp.conj(probe_q)
        sky_rows = sky_all[aimed]
        weight_rows = weights[slot].astype(jnp.float32).reshape(CHANNELS, 1, W, W)
        lifted = sky_rows * delta[None]
        freq_real, freq_imag = transform(to_half(jnp.real(lifted)), to_half(jnp.imag(lifted)), cosine_table, sine_table, False)
        back_real, back_imag = transform(to_half(weight_rows * freq_real), to_half(weight_rows * freq_imag), cosine_table, sine_table, True)
        scale = alive / CHANNELS
        grad_real = lax.optimization_barrier(jnp.sum(sky_rows * back_real, axis=0)) * scale
        grad_imag = lax.optimization_barrier(jnp.sum(sky_rows * back_imag, axis=0)) * scale
        gradient = grad_real + 1j * grad_imag
        gain_p = beam_q * gradient
        gain_q = beam_p * jnp.conj(gradient)

        def add_into(field, station, piece):
            place = (station.astype(jnp.int32), zero_index, row_start, col_start)
            current = lax.dynamic_slice(field, place, (1, 4, W, W))
            return lax.dynamic_update_slice(field, current + piece[None], place)
        out_real = add_into(add_into(out_real, station_p, jnp.real(gain_p)), station_q, jnp.real(gain_q))
        out_imag = add_into(add_into(out_imag, station_p, jnp.imag(gain_p)), station_q, jnp.imag(gain_q))
        return ((out_real, out_imag), None)
    start_real = jnp.zeros((STATIONS, 4, G, G), jnp.float32)
    start_imag = jnp.zeros((STATIONS, 4, G, G), jnp.float32)
    (out_real, out_imag), unused = lax.scan(visit, (start_real, start_imag), jnp.arange(SUBGRIDS, dtype=jnp.int32))
    return jnp.concatenate([out_real, out_imag], axis=1).reshape(STATIONS, 8, G * G)
```

```python
import math

import jax
import jax.numpy as jnp
from jax import lax
from jax.experimental import pallas as pl
from jax.experimental.pallas import tpu as pltpu
from jax.sharding import PartitionSpec as P

G = 64
W = 32
REACH = 2
ST_DEV = 4
SUB_DEV = 32
CH_DEV = 8
POLS = 4
HALVES = 2
GROUP = 4
QUADS = SUB_DEV // GROUP
QUADS_HALF = QUADS // HALVES
PARTS = POLS * HALVES
LANES = GROUP * W
NEAR = 2 * REACH + 1
SMEM = pltpu.SMEM
VMEM = pltpu.VMEM


def shifted(value, axis, by):
    count = lax.axis_size(axis)
    return lax.ppermute(value, axis, [(i, (i + by) % count) for i in range(count)])


def pass_tables():
    position = jnp.arange(W, dtype=jnp.int32)
    product = position[:, None] * position[None, :] % W
    angles = product.astype(jnp.float32) * (2.0 * math.pi / W)
    norm_factor = 1.0 / math.sqrt(W)
    cosine = jnp.cos(angles) * norm_factor
    sine = jnp.sin(angles) * norm_factor
    eye = jnp.eye(GROUP, dtype=jnp.float32)

    def right(sign):
        cos_block, sin_block = jnp.kron(eye, cosine), sign * jnp.kron(eye, sine)
        return jnp.block([[cos_block, sin_block], [-sin_block, cos_block]])

    def left(sign):
        return jnp.kron(eye, jnp.block([[cosine, -sign * sine], [sign * sine, cosine]]))

    return jnp.stack([right(-1.0), left(-1.0), right(1.0), left(1.0)]).astype(jnp.bfloat16)


def swap_halves(value):
    return pltpu.roll(value, G, 1)


def lane_index(rows):
    return lax.broadcasted_iota(jnp.int32, (rows, 2 * G), 1)


def delta_kernel(meta, *refs):
    near, out, wide = refs[:NEAR], refs[NEAR], refs[NEAR + 1]
    half = meta[4, 0]
    for block in range(NEAR):
        wide[pl.ds(block * ST_DEV, ST_DEV)] = near[block][...].astype(jnp.float32)
    lane = lane_index(W)
    for step in range(QUADS_HALF):
        real = jnp.zeros((W, LANES), jnp.float32)
        imag = jnp.zeros((W, LANES), jnp.float32)
        for member in range(GROUP):
            slot = (HALVES * step + half) * GROUP + member
            rows = pl.ds(meta[2, slot], W)
            left = meta[3, slot]
            beam_p = wide[meta[0, slot], 0, rows, :]
            probe_p = wide[meta[0, slot], 1, rows, :]
            beam_q = wide[meta[1, slot], 0, rows, :]
            probe_q = wide[meta[1, slot], 1, rows, :]
            same = probe_p * beam_q + beam_p * probe_q
            cross = probe_p * swap_halves(beam_q) - swap_halves(beam_p) * probe_q
            sum_real = same + swap_halves(same)
            sum_imag = swap_halves(cross) - cross
            shift = lax.rem(member * W + 2 * G - left, 2 * G)
            mine = (lane >= member * W) & (lane < (member + 1) * W)
            real = jnp.where(mine, pltpu.roll(sum_real, shift, 1), real)
            imag = jnp.where(mine, pltpu.roll(sum_imag, shift, 1), imag)
        out[step, 0] = real.astype(jnp.bfloat16)
        out[step, 1] = imag.astype(jnp.bfloat16)


def hessian_kernel(meta, delta, weights, sky, tables, out, sky_wide):
    live = meta[5, 0]
    quads = (live + GROUP - 1) // GROUP
    lane = lane_index(W)
    right_forward, left_forward = tables[0], tables[1]
    right_inverse, left_inverse = tables[2], tables[3]
    wide = jnp.float32
    half_type = jnp.bfloat16

    def dot(a, b):
        return jnp.dot(a, b, preferred_element_type=wide)

    def to_rows(value):
        groups = []
        for group in range(CH_DEV // GROUP):
            pieces = []
            for member in range(GROUP):
                first = (group * GROUP + member) * W
                for part in range(2):
                    pieces.append(value[first : first + W, part * LANES : (part + 1) * LANES])
            groups.append(jnp.concatenate(pieces, axis=0))
        return jnp.concatenate(groups, axis=1)

    def piece(value, channel, part):
        group, member = channel // GROUP, channel % GROUP
        first = (member * 2 + part) * W
        return value[first : first + W, group * LANES : (group + 1) * LANES]

    def visit(quad, carry):
        step, half = quad // HALVES, quad % HALVES
        for channel in range(CH_DEV):
            chosen = sky[meta[6, quad * GROUP], channel].astype(wide)
            for member in range(1, GROUP):
                other = sky[meta[6, quad * GROUP + member], channel].astype(wide)
                chosen = jnp.where(lane >= member * W, other, chosen)
            sky_wide[channel] = chosen
        for pol in range(POLS):
            part_index = pol * HALVES + half
            real = delta[part_index, step, 0].astype(wide)
            imag = delta[part_index, step, 1].astype(wide)
            lifted = jnp.concatenate(
                [
                    jnp.concatenate(
                        [
                            (sky_wide[channel] * real).astype(half_type),
                            (sky_wide[channel] * imag).astype(half_type),
                        ],
                        axis=1,
                    )
                    for channel in range(CH_DEV)
                ],
                axis=0,
            )
            middle = dot(lifted, right_forward).astype(half_type)
            freq = dot(left_forward, to_rows(middle))
            weighted = jnp.concatenate(
                [
                    jnp.concatenate(
                        [
                            (
                                piece(freq, channel, part) * weights[quad, channel].astype(wide)
                            ).astype(half_type)
                            for part in range(2)
                        ],
                        axis=1,
                    )
                    for channel in range(CH_DEV)
                ],
                axis=0,
            )
            middle = dot(weighted, right_inverse).astype(half_type)
            back = dot(left_inverse, to_rows(middle))
            for part in range(2):
                total = sky_wide[0] * piece(back, 0, part)
                for channel in range(1, CH_DEV):
                    total = total + sky_wide[channel] * piece(back, channel, part)
                out[part_index, step, part] = total.astype(half_type)
        return carry

    lax.fori_loop(0, quads, visit, 0)

    def blank(quad, carry):
        for pol in range(POLS):
            out[pol * HALVES + quad % HALVES, quad // HALVES] = jnp.zeros((2, W, LANES), half_type)
        return carry

    lax.fori_loop(quads, QUADS, blank, 0)


def product_kernel(channels_total, meta, grads, *refs):
    near, out, beams, totals = refs[:NEAR], refs[NEAR], refs[NEAR + 1], refs[NEAR + 2]
    half, live = meta[4, 0], meta[5, 0]
    for block in range(NEAR):
        beams[pl.ds(block * ST_DEV, ST_DEV)] = near[block][:, 0].astype(jnp.float32)
    totals[...] = jnp.zeros_like(totals)
    lane = lane_index(W)
    column = lax.rem(lane, G)
    scale = 1.0 / channels_total

    for step in range(QUADS_HALF):
        first = (HALVES * step + half) * GROUP

        @pl.when(first < live)
        def _():
            real = grads[0, step, 0].astype(jnp.float32)
            imag = grads[0, step, 1].astype(jnp.float32)
            for source in range(1, CH_DEV):
                real = real + grads[source, step, 0].astype(jnp.float32)
                imag = imag + grads[source, step, 1].astype(jnp.float32)
            real = real * scale
            imag = imag * scale
            for member in range(GROUP):
                slot = first + member

                @pl.when(slot < live)
                def _():
                    rows = pl.ds(meta[2, slot], W)
                    left = meta[3, slot]
                    station_p, station_q = meta[0, slot], meta[1, slot]
                    low = lax.rem(left + 2 * G - member * W, 2 * G)
                    high = lax.rem(left + 3 * G - member * W, 2 * G)
                    inside = (column >= left) & (column < left + W)
                    upper = lane >= G

                    def placed(value):
                        both = jnp.where(
                            upper, pltpu.roll(value, high, 1), pltpu.roll(value, low, 1)
                        )
                        return jnp.where(inside, both, 0.0)

                    grad_real = placed(real)
                    grad_imag = placed(imag)
                    grad_imag = jnp.where(upper, grad_imag, -grad_imag)
                    beam_p = beams[station_p, rows, :]
                    beam_q = beams[station_q, rows, :]
                    totals[station_p, rows, :] += (
                        beam_q * grad_real + swap_halves(beam_q) * grad_imag
                    )
                    totals[station_q, rows, :] += (
                        beam_p * grad_real - swap_halves(beam_p) * grad_imag
                    )

    for block in range(NEAR):
        out[block] = totals[pl.ds(block * ST_DEV, ST_DEV)].astype(jnp.bfloat16)


def call(kernel, out_shape, in_specs, scratch_shapes):
    return pl.pallas_call(
        kernel,
        out_shape=out_shape,
        in_specs=in_specs,
        out_specs=pl.BlockSpec(memory_space=VMEM),
        scratch_shapes=scratch_shapes,
        compiler_params=pltpu.CompilerParams(vmem_limit_bytes=48 * 1024 * 1024),
    )


def per_device(screens, direction, sky, weights, pairs, pointing, counts):
    base_count = lax.axis_size("base")
    myself = lax.axis_index("base")
    channels_total = CH_DEV * lax.axis_size("chan")
    chunk = lax.axis_index("chan")
    pol, half = chunk // HALVES, chunk % HALVES
    in_smem = pl.BlockSpec(memory_space=SMEM)
    in_vmem = pl.BlockSpec(memory_space=VMEM)

    stacked = jnp.stack([screens, direction], axis=1)
    own = jnp.concatenate(
        [
            lax.dynamic_index_in_dim(stacked, part * POLS + pol, 2, keepdims=False).reshape(
                ST_DEV, 2, G, G
            )
            for part in range(2)
        ],
        axis=-1,
    )
    near = [
        own if by == 0 else shifted(own, "base", -by) for by in range(-REACH, REACH + 1)
    ]

    alive = jnp.arange(SUB_DEV, dtype=jnp.int32) < counts[0]
    local = (pairs // ST_DEV - myself + REACH) % base_count * ST_DEV + pairs % ST_DEV
    local = jnp.where(alive[:, None], local, 0)
    meta = jnp.stack(
        [
            local[:, 0],
            local[:, 1],
            pointing // 4 * (G - W) // 3,
            pointing % 4 * (G - W) // 3,
            jnp.broadcast_to(half, (SUB_DEV,)),
            jnp.broadcast_to(counts[0], (SUB_DEV,)),
            pointing,
        ]
    ).astype(jnp.int32)

    chunk_shape = (QUADS_HALF, 2, W, LANES)
    delta_mine = call(
        delta_kernel,
        jax.ShapeDtypeStruct(chunk_shape, jnp.bfloat16),
        [in_smem] + [in_vmem] * NEAR,
        [pltpu.VMEM((NEAR * ST_DEV, 2, G, 2 * G), jnp.float32)],
    )(meta, *near)
    delta = lax.all_gather(delta_mine, "chan")

    weight_quads = (
        weights.reshape(QUADS, GROUP, CH_DEV, W, W)
        .transpose(0, 2, 3, 1, 4)
        .reshape(QUADS, CH_DEV, W, LANES)
    )
    sky_tiled = jnp.tile(sky.reshape(-1, CH_DEV, W, W), (1, 1, 1, GROUP))
    partial = call(
        hessian_kernel,
        jax.ShapeDtypeStruct((PARTS,) + chunk_shape, jnp.bfloat16),
        [in_smem] + [in_vmem] * 4,
        [pltpu.VMEM((CH_DEV, W, LANES), jnp.float32)],
    )(meta, delta, weight_quads, sky_tiled, pass_tables())
    grads = lax.all_to_all(partial, "chan", 0, 0, tiled=True)

    def make_product(*args):
        return product_kernel(channels_total, *args)

    sums = call(
        make_product,
        jax.ShapeDtypeStruct((NEAR, ST_DEV, G, 2 * G), jnp.bfloat16),
        [in_smem] + [in_vmem] * (1 + NEAR),
        [
            pltpu.VMEM((NEAR * ST_DEV, G, 2 * G), jnp.float32),
            pltpu.VMEM((NEAR * ST_DEV, G, 2 * G), jnp.float32),
        ],
    )(meta, grads, *near)
    mine = sums[REACH].astype(jnp.float32)
    for by in range(-REACH, REACH + 1):
        if by != 0:
            mine = mine + shifted(sums[by + REACH], "base", by).astype(jnp.float32)
    every = lax.all_gather(mine.astype(jnp.bfloat16), "chan")
    every = every.reshape(POLS, HALVES, ST_DEV, G, 2, G).astype(jnp.float32)
    result = every[:, 0] + every[:, 1]
    return result.transpose(1, 3, 0, 2, 4).reshape(ST_DEV, 2 * POLS, G * G)


def solution(mesh):
    in_specs = (
        P("base", None, None),
        P("base", None, None),
        P(None, "chan", None),
        P("base", "chan", None),
        P("base", None),
        P("base"),
        P("base"),
    )
    out_specs = P("base", None, None)
    return jax.shard_map(
        per_device, mesh=mesh, in_specs=in_specs, out_specs=out_specs, check_vma=False
    )
```

```python
import math

import jax
import jax.numpy as jnp
from jax import lax
from jax.experimental import pallas as pl
from jax.experimental.pallas import tpu as pltpu
from jax.sharding import PartitionSpec as P

G = 64
W = 32
REACH = 2
ST_DEV = 4
SUB_DEV = 32
CH_DEV = 8
POLS = 4
HALVES = 2
GROUP = 4
QUADS = SUB_DEV // GROUP
HALF_ROWS = W // HALVES
PARTS = POLS * HALVES
LANES = GROUP * W
NEAR = 2 * REACH + 1
SETS = 2
CHANNELS = SETS * CH_DEV
POLS_DEV = POLS // SETS
SMEM = pltpu.SMEM
VMEM = pltpu.VMEM


def across_chan(value, bit):
    count = lax.axis_size("chan")
    return lax.ppermute(value, "chan", [(i, i ^ bit) for i in range(count)])


def to_sibling(value):
    count = lax.axis_size("base")
    return lax.ppermute(value, "base", [(i, i ^ 1) for i in range(count)])


def turned_half(base, base_count):
    return base * 2 // base_count


def across_chips(value, phase):
    base_count, chan_count = lax.axis_size("base"), lax.axis_size("chan")
    perm = []
    for chan in range(chan_count):
        for base in range(base_count):
            step = 2 if (base // 2 + phase) % 2 == 0 else -2
            target = (base + step) % base_count
            turn = turned_half(base, base_count) ^ turned_half(target, base_count)
            perm.append((chan * base_count + base, (chan ^ (4 * turn)) * base_count + target))
    return lax.ppermute(value, ("chan", "base"), perm)


def pass_tables():
    position = jnp.arange(W, dtype=jnp.int32)
    product = position[:, None] * position[None, :] % W
    angles = product.astype(jnp.float32) * (2.0 * math.pi / W)
    norm_factor = 1.0 / math.sqrt(W)
    cosine = jnp.cos(angles) * norm_factor
    sine = jnp.sin(angles) * norm_factor
    order = jnp.arange(W, dtype=jnp.int32).reshape(8, 4).T[jnp.array([0, 2, 1, 3])].reshape(W)
    cosine_rows, sine_rows = cosine[order][:, order], sine[order][:, order]
    eye = jnp.eye(GROUP, dtype=jnp.float32)

    def right(sign):
        cos_block, sin_block = jnp.kron(eye, cosine), sign * jnp.kron(eye, sine)
        return jnp.block([[cos_block, sin_block], [-sin_block, cos_block]])

    def left(sign):
        return jnp.kron(eye, jnp.block([[cosine_rows, -sign * sine_rows], [sign * sine_rows, cosine_rows]]))

    return jnp.stack([right(-1.0), left(-1.0), right(1.0), left(1.0)]).astype(jnp.bfloat16)


def swap_halves(value):
    return pltpu.roll(value, G, 1)


def lane_index(rows):
    return lax.broadcasted_iota(jnp.int32, (rows, 2 * G), 1)


def prep_kernel(meta, weights, sky, weight_quads, sky_quads, stage, sky_stage):
    wide = jnp.float32
    quads = (meta[5, 0] + GROUP - 1) // GROUP
    lane = lane_index(8)
    low_half = lane < 2 * W
    even_group = lax.rem(lane, 2 * W) < W

    def turned(value, dest):
        for high in range(8):
            dest[pl.ds(high, CH_DEV, stride=8), :] = value[:, high * LANES : (high + 1) * LANES]

    def turn_sky(point, carry):
        turned(sky[point].astype(wide), sky_stage.at[point])
        return carry

    lax.fori_loop(0, sky.shape[0], turn_sky, 0)

    def exchange(first, second, keep, by):
        return (
            jnp.where(keep, first, pltpu.roll(second, by, 1)),
            jnp.where(keep, pltpu.roll(first, LANES - by, 1), second),
        )

    def side_by_side(members):
        a, c = exchange(members[0], members[2], low_half, 2 * W)
        b, d = exchange(members[1], members[3], low_half, 2 * W)
        a, b = exchange(a, b, even_group, W)
        c, d = exchange(c, d, even_group, W)
        return jnp.concatenate([a, c, b, d], axis=0).astype(jnp.bfloat16)

    def visit(quad, carry):
        for member in range(GROUP):
            turned(weights[quad * GROUP + member].astype(wide), stage.at[member])
        points = [meta[6, quad * GROUP + member] for member in range(GROUP)]
        for channel in range(CH_DEV):
            rows = pl.ds(channel * 8, 8)
            weight_quads[quad, channel] = side_by_side(
                [stage[member, rows, :] for member in range(GROUP)]
            )
            sky_quads[quad, channel] = side_by_side(
                [sky_stage[points[member], rows, :] for member in range(GROUP)]
            )
        return carry

    lax.fori_loop(0, quads, visit, 0)


def delta_kernel(meta, own, chip_a, chip_b, sibling, out, wide, turn):
    quads = (meta[5, 0] + GROUP - 1) // GROUP
    for block, value in enumerate((own, chip_a, chip_b, sibling.at[0], sibling.at[1])):
        wide[pl.ds(block * ST_DEV, ST_DEV)] = value[...].astype(jnp.float32)
    lane = lane_index(HALF_ROWS)

    def visit(quad, carry):
        real = jnp.zeros((HALF_ROWS, LANES), jnp.float32)
        imag = jnp.zeros((HALF_ROWS, LANES), jnp.float32)
        for member in range(GROUP):
            slot = quad * GROUP + member
            rows = pl.ds(meta[2, slot], HALF_ROWS)
            left = meta[3, slot]
            beam_p = wide[meta[0, slot], 0, rows, :]
            probe_p = wide[meta[0, slot], 1, rows, :]
            beam_q = wide[meta[1, slot], 0, rows, :]
            probe_q = wide[meta[1, slot], 1, rows, :]
            same = probe_p * beam_q + beam_p * probe_q
            cross = probe_p * swap_halves(beam_q) - swap_halves(beam_p) * probe_q
            sum_real = same + swap_halves(same)
            sum_imag = swap_halves(cross) - cross
            shift = lax.rem(member * W + 2 * G - left, 2 * G)
            mine = (lane >= member * W) & (lane < (member + 1) * W)
            real = jnp.where(mine, pltpu.roll(sum_real, shift, 1), real)
            imag = jnp.where(mine, pltpu.roll(sum_imag, shift, 1), imag)
        for part, value in enumerate((real, imag)):
            turn[part] = value
            out[quad, part] = jnp.concatenate(
                [turn[part, pl.ds(low, 8, stride=2), :] for low in range(2)], axis=0
            ).astype(jnp.bfloat16)
        return carry

    lax.fori_loop(0, quads, visit, 0)


def hessian_kernel(
    meta, mine, over_four, over_two, weights_0, weights_1, sky_0, sky_1, tables, kept, sent
):
    quads = (meta[5, 0] + GROUP - 1) // GROUP
    delta = ((mine, over_four), (over_two.at[0], over_two.at[1]))
    grads = (kept, sent)
    lane = lane_index(HALF_ROWS)
    right_forward, left_forward = tables[0], tables[1]
    right_inverse, left_inverse = tables[2], tables[3]
    wide = jnp.float32
    half_type = jnp.bfloat16

    def weight(quad, channel):
        return (weights_0, weights_1)[channel // CH_DEV][quad, channel % CH_DEV].astype(wide)

    def bright(quad, channel):
        return (sky_0, sky_1)[channel // CH_DEV][quad, channel % CH_DEV].astype(wide)

    def dot(a, b):
        return jnp.dot(a, b, preferred_element_type=wide)

    def to_rows(value):
        groups = []
        for group in range(POLS_DEV * CHANNELS // GROUP):
            pieces = []
            for member in range(GROUP):
                first = (group * GROUP + member) * W
                for part in range(2):
                    pieces.append(value[first : first + W, part * LANES : (part + 1) * LANES])
            groups.append(jnp.concatenate(pieces, axis=0))
        return jnp.concatenate(groups, axis=1)

    def piece(value, pol, channel, part):
        group, member = pol * (CHANNELS // GROUP) + channel // GROUP, channel % GROUP
        first = (member * 2 + part) * W
        return value[first : first + W, group * LANES : (group + 1) * LANES]

    def visit(quad, carry):
        odd = jnp.full((HALF_ROWS, LANES), meta[7, quad * GROUP], jnp.int32)
        for member in range(1, GROUP):
            odd = jnp.where(lane >= member * W, meta[7, quad * GROUP + member], odd)
        odd = odd > 0

        def both_rows(pol, part):
            first, second = (value[quad, part].astype(wide) for value in delta[pol])
            return jnp.concatenate(
                [jnp.where(odd, second, first), jnp.where(odd, first, second)], axis=0
            )

        images = [[both_rows(pol, part) for part in range(2)] for pol in range(POLS_DEV)]
        lifted = jnp.concatenate(
            [
                jnp.concatenate(
                    [
                        (bright(quad, channel) * images[pol][part]).astype(half_type)
                        for part in range(2)
                    ],
                    axis=1,
                )
                for pol in range(POLS_DEV)
                for channel in range(CHANNELS)
            ],
            axis=0,
        )
        middle = dot(lifted, right_forward).astype(half_type)
        freq = dot(left_forward, to_rows(middle))
        weighted = jnp.concatenate(
            [
                jnp.concatenate(
                    [
                        (
                            piece(freq, pol, channel, part) * weight(quad, channel)
                        ).astype(half_type)
                        for part in range(2)
                    ],
                    axis=1,
                )
                for pol in range(POLS_DEV)
                for channel in range(CHANNELS)
            ],
            axis=0,
        )
        middle = dot(weighted, right_inverse).astype(half_type)
        back = dot(left_inverse, to_rows(middle))
        for pol in range(POLS_DEV):
            for part in range(2):
                total = bright(quad, 0) * piece(back, pol, 0, part)
                for channel in range(1, CHANNELS):
                    total = total + bright(quad, channel) * piece(
                        back, pol, channel, part
                    )
                even_rows, odd_rows = total[:HALF_ROWS], total[HALF_ROWS:]
                chunks = (
                    jnp.where(odd, odd_rows, even_rows),
                    jnp.where(odd, even_rows, odd_rows),
                )
                for half in range(HALVES):
                    grads[pol][half, quad, part] = chunks[half].astype(half_type)
        return carry

    lax.fori_loop(0, quads, visit, 0)


def product_kernel(
    channels_total,
    meta,
    kept,
    over_two,
    over_four,
    own,
    chip_a,
    chip_b,
    sibling,
    out_own,
    out_chips,
    out_sibling,
    beams,
    totals,
    turn,
):
    live = meta[5, 0]
    quads = (live + GROUP - 1) // GROUP
    for block, value in enumerate((own, chip_a, chip_b, sibling.at[0], sibling.at[1])):
        beams[pl.ds(block * ST_DEV, ST_DEV)] = value[:, 0].astype(jnp.float32)
    totals[...] = jnp.zeros_like(totals)
    lane = lane_index(HALF_ROWS)
    column = lax.rem(lane, G)
    upper = lane >= G
    scale = 1.0 / channels_total

    def visit(quad, carry):
        for part in range(2):
            total = kept[0, quad, part].astype(jnp.float32)
            total = total + over_two[0, quad, part].astype(jnp.float32)
            total = total + over_four[quad, part].astype(jnp.float32)
            total = total * scale
            for low in range(2):
                turn[part, pl.ds(low, 8, stride=2), :] = total[low * 8 : (low + 1) * 8]
        real, imag = turn[0], turn[1]
        for member in range(GROUP):
            slot = quad * GROUP + member
            rows = pl.ds(meta[2, slot], HALF_ROWS)
            left = meta[3, slot]
            station_p, station_q = meta[0, slot], meta[1, slot]
            low = lax.rem(left + 2 * G - member * W, 2 * G)
            high = lax.rem(left + 3 * G - member * W, 2 * G)
            inside = (column >= left) & (column < left + W) & (slot < live)

            def placed(value):
                both = jnp.where(upper, pltpu.roll(value, high, 1), pltpu.roll(value, low, 1))
                return jnp.where(inside, both, 0.0)

            grad_real = placed(real)
            grad_imag = placed(imag)
            grad_imag = jnp.where(upper, grad_imag, -grad_imag)
            beam_p = beams[station_p, rows, :]
            beam_q = beams[station_q, rows, :]
            totals[station_p, rows, :] += beam_q * grad_real + swap_halves(beam_q) * grad_imag
            totals[station_q, rows, :] += beam_p * grad_real - swap_halves(beam_p) * grad_imag
        return carry

    lax.fori_loop(0, quads, visit, 0)
    out_own[...] = totals[:ST_DEV]
    for block in range(2):
        out_chips[block] = totals[pl.ds((1 + block) * ST_DEV, ST_DEV)]
        out_sibling[block] = totals[pl.ds((3 + block) * ST_DEV, ST_DEV)].astype(jnp.bfloat16)


def result_kernel(meta, mine, over_four, over_two, over_one, out, stage):
    half, low, high = meta[4, 0], meta[9, 0], meta[10, 0]
    lane = lane_index(G // 2)
    lower = lane < G
    own_first = jnp.full((G // 2, 2 * G), half, jnp.int32) == 0
    pairs = (
        (mine, over_four),
        (over_two.at[0], over_two.at[1]),
        (over_one.at[0], over_one.at[1]),
        (over_one.at[2], over_one.at[3]),
    )
    for turn, (same, other) in enumerate(pairs):
        pol = (high ^ (turn // 2)) * 2 + (low ^ (turn % 2))
        for station in range(ST_DEV):
            a = same[station].astype(jnp.float32)
            b = other[station].astype(jnp.float32)
            even, odd = jnp.where(own_first, a, b), jnp.where(own_first, b, a)
            real = jnp.where(lower, even, swap_halves(odd))
            imag = jnp.where(lower, swap_halves(even), odd)
            stage[station, pl.ds(pol, G // 2, stride=2 * POLS), :] = real
            stage[station, pl.ds(pol + POLS, G // 2, stride=2 * POLS), :] = imag
    for station in range(ST_DEV):
        for pair in range(G // 2):
            out[station, :, pair * 2 * G : (pair + 1) * 2 * G] = stage[
                station, pair * 2 * POLS : (pair + 1) * 2 * POLS, :
            ]


def call(kernel, out_shape, in_specs, scratch_shapes):
    return pl.pallas_call(
        kernel,
        out_shape=out_shape,
        in_specs=in_specs,
        out_specs=jax.tree.map(lambda _: pl.BlockSpec(memory_space=VMEM), out_shape),
        scratch_shapes=scratch_shapes,
        compiler_params=pltpu.CompilerParams(vmem_limit_bytes=48 * 1024 * 1024),
    )


def per_device(screens, direction, sky, weights, pairs, pointing, counts):
    base_count = lax.axis_size("base")
    myself = lax.axis_index("base")
    channels_total = CH_DEV * lax.axis_size("chan")
    part = lax.axis_index("chan") ^ (4 * turned_half(myself, base_count))
    pol_high, pol_low, half = part % 2, part // 2 % 2, part // 4
    core, chip_odd = myself % 2, myself // 2 % 2
    in_smem = pl.BlockSpec(memory_space=SMEM)
    in_vmem = pl.BlockSpec(memory_space=VMEM)

    weights_other = across_chan(weights, 1)
    sky_other = across_chan(sky, 1)

    stacked = jnp.stack([screens, direction], axis=1).reshape(ST_DEV, 2, 2, POLS, G // 2, 2, G)
    own = lax.dynamic_index_in_dim(stacked, pol_high * 2 + pol_low, 3, keepdims=False)
    own = lax.dynamic_index_in_dim(own, half, 4, keepdims=False)
    own = jnp.concatenate([own[:, :, 0], own[:, :, 1]], axis=-1)
    chip_a = across_chips(own, 0)
    chip_b = across_chips(own, 1)
    shared_is_a = core == chip_odd
    sibling = to_sibling(jnp.stack([own, jnp.where(shared_is_a, chip_a, chip_b)]))
    near = (own, chip_a, chip_b, sibling)

    alive = jnp.arange(SUB_DEV, dtype=jnp.int32) < counts[0]
    offset = (pairs // ST_DEV - myself + REACH) % base_count - REACH
    block = jnp.where(
        offset == 0,
        0,
        jnp.where(
            jnp.abs(offset) == 2,
            1 + ((offset == 2) == (chip_odd == 1)),
            3 + ((offset == 1) == (core == 1)),
        ),
    )
    local = jnp.where(alive[:, None], block * ST_DEV + pairs % ST_DEV, 0)
    row_start = pointing // 4 * (G - W) // 3

    def spread(value):
        return jnp.broadcast_to(value, (SUB_DEV,))

    meta = jnp.stack(
        [
            local[:, 0],
            local[:, 1],
            (row_start + 1 - half) // 2,
            pointing % 4 * (G - W) // 3,
            spread(half),
            spread(counts[0]),
            pointing,
            row_start % 2 ^ half,
            spread(0),
            spread(pol_low),
            spread(pol_high),
        ]
    ).astype(jnp.int32)

    def prepared(weights, sky):
        quad_shape = (QUADS, CH_DEV, W, LANES)
        return call(
            prep_kernel,
            [jax.ShapeDtypeStruct(quad_shape, jnp.bfloat16)] * 2,
            [in_smem] + [in_vmem] * 2,
            [
                pltpu.VMEM((GROUP, CH_DEV * 8, LANES), jnp.float32),
                pltpu.VMEM((sky.shape[0], CH_DEV * 8, LANES), jnp.float32),
            ],
        )(meta, weights, sky)

    weights_0, sky_0 = prepared(weights, sky)
    weights_1, sky_1 = prepared(weights_other, sky_other)

    chunk_shape = (QUADS, 2, HALF_ROWS, LANES)
    turn = pltpu.VMEM((2, HALF_ROWS, LANES), jnp.float32)
    delta = call(
        delta_kernel,
        jax.ShapeDtypeStruct(chunk_shape, jnp.bfloat16),
        [in_smem] + [in_vmem] * len(near),
        [pltpu.VMEM((NEAR * ST_DEV, 2, G // 2, 2 * G), jnp.float32), turn],
    )(meta, *near)
    over_four = across_chan(delta, 4)
    over_two = across_chan(jnp.stack([delta, over_four]), 2)

    kept, sent = call(
        hessian_kernel,
        [jax.ShapeDtypeStruct((HALVES,) + chunk_shape, jnp.bfloat16)] * 2,
        [in_smem] + [in_vmem] * 8,
        [],
    )(
        meta, delta, over_four, over_two, weights_0, weights_1, sky_0, sky_1, pass_tables()
    )
    wide = jnp.float32
    back_two = across_chan(sent, 2)
    other_half = kept[1].astype(wide) + back_two[1].astype(wide)
    back_four = across_chan(other_half.astype(jnp.bfloat16), 4)

    def make_product(*args):
        return product_kernel(channels_total, *args)

    table = pltpu.VMEM((NEAR * ST_DEV, G // 2, 2 * G), wide)
    block_shape = (ST_DEV, G // 2, 2 * G)
    sum_own, sum_chips, sum_sibling = call(
        make_product,
        [
            jax.ShapeDtypeStruct(block_shape, wide),
            jax.ShapeDtypeStruct((2,) + block_shape, wide),
            jax.ShapeDtypeStruct((2,) + block_shape, jnp.bfloat16),
        ],
        [in_smem] + [in_vmem] * (3 + len(near)),
        [table, table, turn],
    )(meta, kept, back_two, back_four, *near)
    from_sibling = to_sibling(sum_sibling).astype(wide)
    sum_a = sum_chips[0] + jnp.where(shared_is_a, from_sibling[1], 0.0)
    sum_b = sum_chips[1] + jnp.where(shared_is_a, 0.0, from_sibling[1])
    from_b = across_chips(sum_b.astype(jnp.bfloat16), 1)
    from_a = across_chips(sum_a.astype(jnp.bfloat16), 0)
    mine = sum_own + from_sibling[0] + from_a.astype(wide) + from_b.astype(wide)
    mine = mine.astype(jnp.bfloat16)
    over_four = across_chan(mine, 4)
    pair = jnp.stack([mine, over_four])
    over_two = across_chan(pair, 2)
    over_one = across_chan(jnp.concatenate([pair, over_two]), 1)
    return call(
        result_kernel,
        jax.ShapeDtypeStruct((ST_DEV, 2 * POLS, G * G), wide),
        [in_smem] + [in_vmem] * 4,
        [pltpu.VMEM((ST_DEV, G // 2 * 2 * POLS, 2 * G), wide)],
    )(meta, mine, over_four, over_two, over_one)


def solution(mesh):
    in_specs = (
        P("base", None, None),
        P("base", None, None),
        P(None, "chan", None),
        P("base", "chan", None),
        P("base", None),
        P("base"),
        P("base"),
    )
    out_specs = P("base", None, None)
    return jax.shard_map(
        per_device, mesh=mesh, in_specs=in_specs, out_specs=out_specs, check_vma=False
    )
```

```python
import functools
import math

import jax
import jax.numpy as jnp
import ml_dtypes
import numpy as np
from jax import lax
from jax.experimental import pallas as pl
from jax.experimental.pallas import tpu as pltpu
from jax.sharding import PartitionSpec as P

G = 64
W = 32
REACH = 2
ST_DEV = 4
SUB_DEV = 32
CH_DEV = 8
POLS = 4
HALVES = 2
GROUP = 4
QUADS = SUB_DEV // GROUP
HALF_ROWS = W // HALVES
PARTS = POLS * HALVES
LANES = GROUP * W
NEAR = 2 * REACH + 1
QUADS_STEP = 4
SETS = 2
SMEM = pltpu.SMEM
VMEM = pltpu.VMEM


def across_chan(value, bit):
    count = lax.axis_size("chan")
    return lax.ppermute(value, "chan", [(i, i ^ bit) for i in range(count)])


def to_sibling(value):
    count = lax.axis_size("base")
    return lax.ppermute(value, "base", [(i, i ^ 1) for i in range(count)])


def turned_half(base, base_count):
    return base * 2 // base_count


def across_chips(value, phase):
    base_count, chan_count = lax.axis_size("base"), lax.axis_size("chan")
    perm = []
    for chan in range(chan_count):
        for base in range(base_count):
            step = 2 if (base // 2 + phase) % 2 == 0 else -2
            target = (base + step) % base_count
            turn = turned_half(base, base_count) ^ turned_half(target, base_count)
            perm.append((chan * base_count + base, (chan ^ (4 * turn)) * base_count + target))
    return lax.ppermute(value, ("chan", "base"), perm)


def pass_tables():
    position = np.arange(W, dtype=np.int32)
    product = position[:, None] * position[None, :] % W
    angles = product.astype(np.float32) * np.float32(2.0 * math.pi / W)
    norm_factor = np.float32(1.0 / math.sqrt(W))
    cosine = np.cos(angles) * norm_factor
    sine = np.sin(angles) * norm_factor
    order = np.arange(W).reshape(8, 4).T[[0, 2, 1, 3]].reshape(W)
    cosine_rows, sine_rows = cosine[order][:, order], sine[order][:, order]
    eye = np.eye(GROUP, dtype=np.float32)

    def right(sign):
        cos_block, sin_block = np.kron(eye, cosine), sign * np.kron(eye, sine)
        return np.block([[cos_block, sin_block], [-sin_block, cos_block]])

    def left(sign):
        turn = np.block([[cosine_rows, -sign * sine_rows], [sign * sine_rows, cosine_rows]])
        return np.kron(eye, turn)

    tables = np.stack([right(-1.0), left(-1.0), right(1.0), left(1.0)])
    return jnp.asarray(tables.astype(ml_dtypes.bfloat16))


def swap_halves(value):
    return pltpu.roll(value, G, 1)


def lane_index(rows):
    return lax.broadcasted_iota(jnp.int32, (rows, 2 * G), 1)


def to_row_order(value, dest):
    for high in range(8):
        dest[pl.ds(high, CH_DEV, stride=8), :] = value[:, high * LANES : (high + 1) * LANES]


def exchange(first, second, keep, by):
    return (
        jnp.where(keep, first, pltpu.roll(second, by, 1)),
        jnp.where(keep, pltpu.roll(first, LANES - by, 1), second),
    )


def side_by_side(members):
    lane = lane_index(8)
    low_half = lane < 2 * W
    even_group = lax.rem(lane, 2 * W) < W
    a, c = exchange(members[0], members[2], low_half, 2 * W)
    b, d = exchange(members[1], members[3], low_half, 2 * W)
    a, b = exchange(a, b, even_group, W)
    c, d = exchange(c, d, even_group, W)
    return jnp.concatenate([a, c, b, d], axis=0).astype(jnp.bfloat16)


def weights_kernel(meta, weights, out, stage):
    def visit(quad, carry):
        for member in range(GROUP):
            value = weights[quad * GROUP + member].astype(jnp.float32)
            to_row_order(value, stage.at[member])
        for channel in range(CH_DEV):
            rows = pl.ds(channel * 8, 8)
            out[quad, channel] = side_by_side([stage[member, rows, :] for member in range(GROUP)])
        return carry

    lax.fori_loop(0, (meta[5, 0] + GROUP - 1) // GROUP, visit, 0)


def sky_kernel(first, meta, sky, out, stage):
    def turn(point, carry):
        to_row_order(sky[first + point].astype(jnp.float32), stage.at[point])
        return carry

    lax.fori_loop(0, stage.shape[0], turn, 0)

    def visit(quad, carry):
        points = [meta[6, quad * GROUP + member] for member in range(GROUP)]
        for channel in range(CH_DEV):
            rows = pl.ds(channel * 8, 8)
            out[quad, channel] = side_by_side([stage[point, rows, :] for point in points])
        return carry

    lax.fori_loop(0, (meta[5, 0] + GROUP - 1) // GROUP, visit, 0)


def own_kernel(screens, direction, out, stage):
    chan = lax.axis_index("chan")
    pol = chan % 2 * 2 + chan // 2 % 2
    lower = lane_index(G // 2) < G
    for station in range(ST_DEV):
        for kind, source in enumerate((screens, direction)):
            value = source[station].astype(jnp.float32)
            spot = stage.at[station * 2 + kind]
            for pair in range(G // 2):
                spot[pair * 2 * POLS : (pair + 1) * 2 * POLS, :] = value[
                    :, pair * 2 * G : (pair + 1) * 2 * G
                ]
            real = spot[pl.ds(pol, G // 2, stride=2 * POLS), :]
            imag = spot[pl.ds(pol + POLS, G // 2, stride=2 * POLS), :]
            even = jnp.where(lower, real, swap_halves(imag))
            odd = jnp.where(lower, swap_halves(real), imag)
            out[station, kind, 0] = even.astype(jnp.bfloat16)
            out[station, kind, 1] = odd.astype(jnp.bfloat16)


def group_index(rows):
    return lane_index(rows) // W


def delta_kernel(meta, own, chip_a, chip_b, sibling, out, beams, turned, probes, turn):
    quads = (meta[5, 0] + GROUP - 1) // GROUP
    for block, value in enumerate((own, chip_a, chip_b, sibling.at[0], sibling.at[1])):
        for member in range(ST_DEV):
            station = block * ST_DEV + member
            for half in range(HALVES):
                beam = value[member, 0, half].astype(jnp.float32)
                beams[station, half] = beam
                probes[station, half] = value[member, 1, half].astype(jnp.float32)
                turned[station, half] = swap_halves(beam)
    group = group_index(HALF_ROWS)

    def visit(quad, carry):
        for half in range(HALVES):
            same = [jnp.zeros((HALF_ROWS, LANES), jnp.float32)] * 2
            cross = [jnp.zeros((HALF_ROWS, LANES), jnp.float32)] * 2
            for member in range(GROUP):
                slot = quad * GROUP + member
                rows = pl.ds(meta[(2, 4)[half], slot], HALF_ROWS)
                station_p, station_q = meta[0, slot], meta[1, slot]
                probe_p = probes[station_p, half, rows, :]
                probe_q = probes[station_q, half, rows, :]
                beam_p = beams[station_p, half, rows, :]
                beam_q = beams[station_q, half, rows, :]
                sum_same = probe_p * beam_q + beam_p * probe_q
                sum_cross = (
                    probe_p * turned[station_q, half, rows, :]
                    - turned[station_p, half, rows, :] * probe_q
                )
                shift = lax.rem(member * W + 2 * G - meta[3, slot], 2 * G)
                sum_same = pltpu.roll(sum_same, shift, 1)
                sum_cross = pltpu.roll(sum_cross, shift, 1)
                for place in range(2):
                    mine = group == (member + 2 * place) % GROUP
                    same[place] = jnp.where(mine, sum_same, same[place])
                    cross[place] = jnp.where(mine, sum_cross, cross[place])
            real = same[0] + swap_halves(same[1])
            imag = swap_halves(cross[1]) - cross[0]
            for part, value in enumerate((real, imag)):
                turn[half, part] = value
                out[quad, part, half] = jnp.concatenate(
                    [turn[half, part, pl.ds(low, 8, stride=2), :] for low in range(2)], axis=0
                ).astype(jnp.bfloat16)
        return carry

    lax.fori_loop(0, quads, visit, 0)


def hessian_kernel(meta, delta, weights_0, weights_1, sky_0, sky_1, tables, out):
    quads = (meta[5, 0] + GROUP - 1) // GROUP
    lane = lane_index(HALF_ROWS)
    right_forward, left_forward = tables[0], tables[1]
    right_inverse, left_inverse = tables[2], tables[3]
    wide = jnp.float32
    half_type = jnp.bfloat16
    channels = SETS * CH_DEV
    images = [(member, channel) for member in range(QUADS_STEP) for channel in range(channels)]

    def weight(quad, channel):
        return (weights_0, weights_1)[channel // CH_DEV][quad, channel % CH_DEV]

    def bright(quad, channel):
        return (sky_0, sky_1)[channel // CH_DEV][quad, channel % CH_DEV]

    def dot(a, b):
        return jnp.dot(a, b, preferred_element_type=wide)

    def to_rows(value):
        groups = []
        for group in range(len(images) // GROUP):
            pieces = []
            for member in range(GROUP):
                first = (group * GROUP + member) * W
                for part in range(2):
                    pieces.append(value[first : first + W, part * LANES : (part + 1) * LANES])
            groups.append(jnp.concatenate(pieces, axis=0))
        return jnp.concatenate(groups, axis=1)

    def piece(value, image, part):
        group, member = image // GROUP, image % GROUP
        first = (member * 2 + part) * W
        return value[first : first + W, group * LANES : (group + 1) * LANES]

    def both_parts(make):
        return jnp.concatenate(
            [
                jnp.concatenate([make(image, part) for part in range(2)], axis=1)
                for image in range(len(images))
            ],
            axis=0,
        )

    def visit(step, carry):
        quad_of = [step * QUADS_STEP + member for member in range(QUADS_STEP)]
        odd = []
        for quad in quad_of:
            value = jnp.full((HALF_ROWS, LANES), meta[7, quad * GROUP], jnp.int32)
            for member in range(1, GROUP):
                value = jnp.where(lane >= member * W, meta[7, quad * GROUP + member], value)
            odd.append(value > 0)

        def both_rows(member, part):
            first, second = (
                delta[quad_of[member], part, half].astype(wide) for half in range(HALVES)
            )
            rows = [
                jnp.where(odd[member], second, first),
                jnp.where(odd[member], first, second),
            ]
            return jnp.concatenate(rows, axis=0).astype(half_type)

        fields = [
            [both_rows(member, part) for part in range(2)] for member in range(QUADS_STEP)
        ]

        def lift(image, part):
            member, channel = images[image]
            return bright(quad_of[member], channel) * fields[member][part]

        middle = dot(both_parts(lift), right_forward).astype(half_type)
        freq = dot(left_forward, to_rows(middle))

        def weigh(image, part):
            member, channel = images[image]
            factor = weight(quad_of[member], channel).astype(wide)
            return (piece(freq, image, part) * factor).astype(half_type)

        middle = dot(both_parts(weigh), right_inverse).astype(half_type)
        back = dot(left_inverse, to_rows(middle))
        for member, quad in enumerate(quad_of):
            for part in range(2):
                total = None
                for channel in range(channels):
                    term = bright(quad, channel).astype(wide) * piece(
                        back, images.index((member, channel)), part
                    )
                    total = term if total is None else total + term
                even_rows, odd_rows = total[:HALF_ROWS], total[HALF_ROWS:]
                chunks = (
                    jnp.where(odd[member], odd_rows, even_rows),
                    jnp.where(odd[member], even_rows, odd_rows),
                )
                for half in range(HALVES):
                    out[quad, part, half] = chunks[half].astype(half_type)
        return carry

    lax.fori_loop(0, (quads + QUADS_STEP - 1) // QUADS_STEP, visit, 0)


def product_kernel(
    channels_total,
    meta,
    kept,
    over_two,
    beams,
    turned,
    out_own,
    out_chips,
    out_sibling,
    totals,
    turn,
):
    live = meta[5, 0]
    quads = (live + GROUP - 1) // GROUP
    totals[...] = jnp.zeros_like(totals)
    group = group_index(HALF_ROWS)
    scale = 1.0 / channels_total

    def visit(quad, carry):
        for half in range(HALVES):
            for part in range(2):
                total = kept[quad, part, half].astype(jnp.float32)
                total = total + over_two[quad, part, half].astype(jnp.float32)
                total = total * scale
                for low in range(2):
                    turn[half, part, pl.ds(low, 8, stride=2), :] = total[low * 8 : (low + 1) * 8]
        for half in range(HALVES):
            real, imag = turn[half, 0], turn[half, 1]
            real_high, imag_high = swap_halves(real), swap_halves(imag)
            for member in range(GROUP):
                slot = quad * GROUP + member
                rows = pl.ds(meta[(2, 4)[half], slot], HALF_ROWS)
                station_p, station_q = meta[0, slot], meta[1, slot]
                shift = lax.rem(meta[3, slot] + 2 * G - member * W, 2 * G)
                alive = slot < live
                low = (group == member) & alive
                high = (group == (member + 2) % GROUP) & alive
                grad_real = jnp.where(low, real, jnp.where(high, real_high, 0.0))
                grad_imag = jnp.where(low, -imag, jnp.where(high, imag_high, 0.0))
                grad_real = pltpu.roll(grad_real, shift, 1)
                grad_imag = pltpu.roll(grad_imag, shift, 1)
                totals[station_p, half, rows, :] += (
                    beams[station_q, half, rows, :] * grad_real
                    + turned[station_q, half, rows, :] * grad_imag
                )
                totals[station_q, half, rows, :] += (
                    beams[station_p, half, rows, :] * grad_real
                    - turned[station_p, half, rows, :] * grad_imag
                )
        return carry

    lax.fori_loop(0, quads, visit, 0)
    out_own[...] = totals[:ST_DEV]
    for block in range(2):
        out_chips[block] = totals[pl.ds((1 + block) * ST_DEV, ST_DEV)]
        out_sibling[block] = totals[pl.ds((3 + block) * ST_DEV, ST_DEV)].astype(jnp.bfloat16)


def result_kernel(mine, over_two, over_one, out, stage):
    chan = lax.axis_index("chan")
    high, low = chan % 2, chan // 2 % 2
    lower = lane_index(G // 2) < G
    for turn, value in enumerate((mine, over_two, over_one.at[0], over_one.at[1])):
        pol = (high ^ (turn // 2)) * 2 + (low ^ (turn % 2))
        for station in range(ST_DEV):
            even = value[station, 0].astype(jnp.float32)
            odd = value[station, 1].astype(jnp.float32)
            real = jnp.where(lower, even, swap_halves(odd))
            imag = jnp.where(lower, swap_halves(even), odd)
            stage[station, pl.ds(pol, G // 2, stride=2 * POLS), :] = real
            stage[station, pl.ds(pol + POLS, G // 2, stride=2 * POLS), :] = imag
    for station in range(ST_DEV):
        for pair in range(G // 2):
            out[station, :, pair * 2 * G : (pair + 1) * 2 * G] = stage[
                station, pair * 2 * POLS : (pair + 1) * 2 * POLS, :
            ]


def call(kernel, out_shape, in_specs, scratch_shapes):
    return pl.pallas_call(
        kernel,
        out_shape=out_shape,
        in_specs=in_specs,
        out_specs=jax.tree.map(lambda _: pl.BlockSpec(memory_space=VMEM), out_shape),
        scratch_shapes=scratch_shapes,
        compiler_params=pltpu.CompilerParams(vmem_limit_bytes=48 * 1024 * 1024),
    )


def per_device(screens, direction, sky, weights, pairs, pointing, counts):
    base_count = lax.axis_size("base")
    myself = lax.axis_index("base")
    channels_total = CH_DEV * lax.axis_size("chan")
    core, chip_odd = myself % 2, myself // 2 % 2
    in_smem = pl.BlockSpec(memory_space=SMEM)
    in_vmem = pl.BlockSpec(memory_space=VMEM)

    alive = jnp.arange(SUB_DEV, dtype=jnp.int32) < counts[0]
    offset = (pairs // ST_DEV - myself + REACH) % base_count - REACH
    block = jnp.where(
        offset == 0,
        0,
        jnp.where(
            jnp.abs(offset) == 2,
            1 + ((offset == 2) == (chip_odd == 0)),
            3 + ((offset == 1) == (core == 1)),
        ),
    )
    local = jnp.where(alive[:, None], block * ST_DEV + pairs % ST_DEV, 0)
    row_start = pointing // 4 * (G - W) // 3

    def spread(value):
        return jnp.broadcast_to(value, (SUB_DEV,))

    meta = jnp.stack(
        [
            local[:, 0],
            local[:, 1],
            (row_start + 1) // 2,
            pointing % 4 * (G - W) // 3,
            row_start // 2,
            spread(counts[0]),
            pointing,
            row_start % 2,
        ]
    ).astype(jnp.int32)

    own = call(
        own_kernel,
        jax.ShapeDtypeStruct((ST_DEV, 2, HALVES, G // 2, 2 * G), jnp.bfloat16),
        [in_vmem] * 2,
        [pltpu.VMEM((2 * ST_DEV, G * POLS, 2 * G), jnp.float32)],
    )(screens, direction)
    chip_a = across_chips(own, 1)
    chip_b = across_chips(own, 0)
    other = across_chan(jnp.concatenate([weights, sky]), 1)
    shared_is_a = core != chip_odd
    sibling = to_sibling(jnp.stack([own, jnp.where(shared_is_a, chip_a, chip_b)]))

    delta_shape = (QUADS, 2, HALVES, HALF_ROWS, LANES)
    turn = pltpu.VMEM((HALVES, 2, HALF_ROWS, LANES), jnp.float32)
    field_shape = (NEAR * ST_DEV, HALVES, G // 2, 2 * G)
    field = pltpu.VMEM(field_shape, jnp.float32)
    delta, beams, turned = call(
        delta_kernel,
        [jax.ShapeDtypeStruct(delta_shape, jnp.bfloat16)]
        + [jax.ShapeDtypeStruct(field_shape, jnp.float32)] * 2,
        [in_smem] + [in_vmem] * 4,
        [field, turn],
    )(meta, own, chip_a, chip_b, sibling)
    over_two = across_chan(delta, 2)
    wide = jnp.float32
    tables = pass_tables()
    quad_shape = jax.ShapeDtypeStruct((QUADS, CH_DEV, W, LANES), jnp.bfloat16)

    def turned_sky(value, first):
        stage = pltpu.VMEM((sky.shape[0], CH_DEV * 8, LANES), wide)
        kernel = functools.partial(sky_kernel, first)
        return call(kernel, quad_shape, [in_smem, in_vmem], [stage])(meta, value)

    def turned_weights(value):
        stage = pltpu.VMEM((GROUP, CH_DEV * 8, LANES), wide)
        return call(weights_kernel, quad_shape, [in_smem, in_vmem], [stage])(meta, value)

    weighting = (turned_weights(weights), turned_weights(other))
    brightness = (turned_sky(sky, 0), turned_sky(other, SUB_DEV))

    def hessian(delta):
        return call(
            hessian_kernel,
            jax.ShapeDtypeStruct(delta_shape, jnp.bfloat16),
            [in_smem] + [in_vmem] * 6,
            [],
        )(meta, delta, *weighting, *brightness, tables)

    sent, delta = lax.optimization_barrier((hessian(over_two), delta))
    back_two = across_chan(sent, 2)
    kept = hessian(delta)

    def make_product(*args):
        return product_kernel(channels_total, *args)

    block_shape = (ST_DEV, HALVES, G // 2, 2 * G)
    sum_own, sum_chips, sum_sibling = call(
        make_product,
        [
            jax.ShapeDtypeStruct(block_shape, wide),
            jax.ShapeDtypeStruct((2,) + block_shape, wide),
            jax.ShapeDtypeStruct((2,) + block_shape, jnp.bfloat16),
        ],
        [in_smem] + [in_vmem] * 4,
        [field, turn],
    )(meta, kept, back_two, beams, turned)
    from_sibling = to_sibling(sum_sibling).astype(wide)
    sum_a = sum_chips[0] + jnp.where(shared_is_a, from_sibling[1], 0.0)
    sum_b = sum_chips[1] + jnp.where(shared_is_a, 0.0, from_sibling[1])
    from_a = across_chips(sum_a.astype(jnp.bfloat16), 1)
    from_b = across_chips(sum_b.astype(jnp.bfloat16), 0)
    mine = sum_own + from_sibling[0] + from_a.astype(wide) + from_b.astype(wide)
    mine = mine.astype(jnp.bfloat16)
    other = across_chan(mine, 4)
    mine = (mine.astype(wide) + other.astype(wide)).astype(jnp.bfloat16)
    over_two = across_chan(mine, 2)
    over_one = across_chan(jnp.stack([mine, over_two]), 1)
    return call(
        result_kernel,
        jax.ShapeDtypeStruct((ST_DEV, 2 * POLS, G * G), wide),
        [in_vmem] * 3,
        [pltpu.VMEM((ST_DEV, G // 2 * 2 * POLS, 2 * G), wide)],
    )(mine, over_two, over_one)


def solution(mesh):
    in_specs = (
        P("base", None, None),
        P("base", None, None),
        P(None, "chan", None),
        P("base", "chan", None),
        P("base", None),
        P("base"),
        P("base"),
    )
    out_specs = P("base", None, None)
    return jax.shard_map(
        per_device, mesh=mesh, in_specs=in_specs, out_specs=out_specs, check_vma=False
    )
```

```python
import functools
import math

import jax
import jax.numpy as jnp
import ml_dtypes
import numpy as np
from jax import lax
from jax.experimental import pallas as pl
from jax.experimental.pallas import tpu as pltpu
from jax.sharding import PartitionSpec as P

G = 64
W = 32
REACH = 2
ST_DEV = 4
SUB_DEV = 32
CH_DEV = 8
POLS = 4
HALVES = 2
GROUP = 4
QUADS = SUB_DEV // GROUP
HALF_ROWS = W // HALVES
PARTS = POLS * HALVES
LANES = GROUP * W
NEAR = 2 * REACH + 1
QUADS_STEP = 4
SETS = 2
SMEM = pltpu.SMEM
VMEM = pltpu.VMEM


def across_chan(value, bit):
    count = lax.axis_size("chan")
    return lax.ppermute(value, "chan", [(i, i ^ bit) for i in range(count)])


def to_sibling(value):
    count = lax.axis_size("base")
    return lax.ppermute(value, "base", [(i, i ^ 1) for i in range(count)])


def turned_half(base, base_count):
    return base * 2 // base_count


def across_chips(value, phase):
    base_count, chan_count = lax.axis_size("base"), lax.axis_size("chan")
    perm = []
    for chan in range(chan_count):
        for base in range(base_count):
            step = 2 if (base // 2 + phase) % 2 == 0 else -2
            target = (base + step) % base_count
            turn = turned_half(base, base_count) ^ turned_half(target, base_count)
            perm.append((chan * base_count + base, (chan ^ (4 * turn)) * base_count + target))
    return lax.ppermute(value, ("chan", "base"), perm)


def pass_tables():
    position = np.arange(W, dtype=np.int32)
    product = position[:, None] * position[None, :] % W
    angles = product.astype(np.float32) * np.float32(2.0 * math.pi / W)
    norm_factor = np.float32(1.0 / math.sqrt(W))
    cosine = np.cos(angles) * norm_factor
    sine = np.sin(angles) * norm_factor
    order = np.arange(W).reshape(8, 4).T[[0, 2, 1, 3]].reshape(W)
    cosine_rows, sine_rows = cosine[order][:, order], sine[order][:, order]
    eye = np.eye(GROUP, dtype=np.float32)

    def right(sign):
        cos_block, sin_block = np.kron(eye, cosine), sign * np.kron(eye, sine)
        return np.block([[cos_block, sin_block], [-sin_block, cos_block]])

    def left(sign):
        turn = np.block([[cosine_rows, -sign * sine_rows], [sign * sine_rows, cosine_rows]])
        return np.kron(eye, turn)

    tables = np.stack([right(-1.0), left(-1.0), right(1.0), left(1.0)])
    return jnp.asarray(tables.astype(ml_dtypes.bfloat16))


def swap_halves(value):
    return pltpu.roll(value, G, 1)


def lane_index(rows):
    return lax.broadcasted_iota(jnp.int32, (rows, 2 * G), 1)


def slots_kernel(pairs, pointing, counts, out):
    base_count = lax.axis_size("base")
    myself = lax.axis_index("base")
    core, chip_odd = lax.rem(myself, 2), lax.rem(myself // 2, 2)
    live = counts[0]
    slot = lax.broadcasted_iota(jnp.int32, (2, SUB_DEV), 1)
    station = pairs[...]
    offset = (station >> 2) - myself
    offset = jnp.where(offset > base_count // 2, offset - base_count, offset)
    offset = jnp.where(offset < -(base_count // 2), offset + base_count, offset)
    two_away = jnp.where((offset > 0) == (chip_odd == 0), 1, 2)
    one_away = jnp.where((offset > 0) == (core == 1), 4, 3)
    far = jnp.abs(offset) == 2
    block = jnp.where(offset == 0, 0, jnp.where(far, two_away, one_away))
    place = jnp.where(slot < live, block * ST_DEV + (station & (ST_DEV - 1)), 0)
    out[0:2, :] = place
    point = pointing[...]

    def start(index):
        value = jnp.zeros_like(index)
        for step in range(1, 4):
            value = jnp.where(index == step, step * (G - W) // 3, value)
        return value

    row = start(point >> 2)
    out[2:3, :] = (row + 1) >> 1
    out[3:4, :] = start(point & 3)
    out[4:5, :] = row >> 1
    out[5:6, :] = jnp.full((1, SUB_DEV), live, jnp.int32)
    out[6:7, :] = point
    out[7:8, :] = row & 1


def group_table():
    place = np.arange(GROUP * LANES).reshape(GROUP, GROUP, W).transpose(1, 0, 2).reshape(-1)
    return jnp.asarray(np.eye(GROUP * LANES)[:, place].astype(ml_dtypes.bfloat16))


def prepare_kernel(first, meta, weights, sky, table, weight_out, sky_out, stage, sky_stage):
    def store(value, dest):
        for high in range(8):
            dest[high * CH_DEV : (high + 1) * CH_DEV, :] = value[
                :, high * LANES : (high + 1) * LANES
            ]

    def side_by_side(stages):
        return jnp.concatenate(
            [
                jnp.concatenate(
                    [
                        stages(quad * GROUP + member)[pl.ds(channel, 8, stride=CH_DEV), :]
                        for member in range(GROUP)
                    ],
                    axis=1,
                )
                for quad in range(QUADS)
                for channel in range(CH_DEV)
            ],
            axis=0,
        ).astype(jnp.bfloat16)

    def write(moved, out):
        for quad in range(QUADS):
            for channel in range(CH_DEV):
                rows = (quad * CH_DEV + channel) * 8
                out[quad, channel] = jnp.concatenate(
                    [
                        moved[rows : rows + 8, low * LANES : (low + 1) * LANES]
                        for low in (0, 2, 1, 3)
                    ],
                    axis=0,
                ).astype(jnp.bfloat16)

    for slot in range(SUB_DEV):
        store(weights[slot].astype(jnp.float32), stage.at[slot])
    for point in range(sky_stage.shape[0]):
        store(sky[first + point].astype(jnp.float32), sky_stage.at[point])
    mover = table[...]
    moved = jnp.dot(
        side_by_side(lambda slot: stage.at[slot]), mover, preferred_element_type=jnp.float32
    )
    write(moved, weight_out)
    moved = jnp.dot(
        side_by_side(lambda slot: sky_stage.at[meta[6, slot]]),
        mover,
        preferred_element_type=jnp.float32,
    )
    write(moved, sky_out)


def own_kernel(screens, direction, out, stage):
    chan = lax.axis_index("chan")
    pol = chan % 2 * 2 + chan // 2 % 2
    lower = lane_index(G // 2) < G
    for station in range(ST_DEV):
        for kind, source in enumerate((screens, direction)):
            value = source[station].astype(jnp.float32)
            spot = stage.at[station * 2 + kind]
            for pair in range(G // 2):
                spot[pair * 2 * POLS : (pair + 1) * 2 * POLS, :] = value[
                    :, pair * 2 * G : (pair + 1) * 2 * G
                ]
            real = spot[pl.ds(pol, G // 2, stride=2 * POLS), :]
            imag = spot[pl.ds(pol + POLS, G // 2, stride=2 * POLS), :]
            even = jnp.where(lower, real, swap_halves(imag))
            odd = jnp.where(lower, swap_halves(real), imag)
            out[station, kind, 0] = even.astype(jnp.bfloat16)
            out[station, kind, 1] = odd.astype(jnp.bfloat16)


def group_index(rows):
    return lane_index(rows) // W


def delta_kernel(
    meta, own, chip_a, chip_b, sibling, out, beams, turned, probes, turn
):
    quads = (meta[5, 0] + GROUP - 1) // GROUP
    for block, value in enumerate((own, chip_a, chip_b, sibling.at[0], sibling.at[1])):
        for member in range(ST_DEV):
            station = block * ST_DEV + member
            for half in range(HALVES):
                beam = value[member, 0, half].astype(jnp.float32)
                beams[station, half] = beam
                probes[station, half] = value[member, 1, half].astype(jnp.float32)
                turned[station, half] = swap_halves(beam)
    group = group_index(HALF_ROWS)

    def visit(step, carry):
        for half, later in [(half, later) for half in range(HALVES) for later in range(2)]:
            quad = 2 * step + later
            same = [jnp.zeros((HALF_ROWS, LANES), jnp.float32)] * 2
            cross = [jnp.zeros((HALF_ROWS, LANES), jnp.float32)] * 2
            for member in range(GROUP):
                slot = quad * GROUP + member
                rows = pl.ds(meta[(2, 4)[half], slot], HALF_ROWS)
                station_p, station_q = meta[0, slot], meta[1, slot]
                probe_p = probes[station_p, half, rows, :]
                probe_q = probes[station_q, half, rows, :]
                beam_p = beams[station_p, half, rows, :]
                beam_q = beams[station_q, half, rows, :]
                sum_same = probe_p * beam_q + beam_p * probe_q
                sum_cross = (
                    probe_p * turned[station_q, half, rows, :]
                    - turned[station_p, half, rows, :] * probe_q
                )
                shift = lax.rem(member * W + 2 * G - meta[3, slot], 2 * G)
                sum_same = pltpu.roll(sum_same, shift, 1)
                sum_cross = pltpu.roll(sum_cross, shift, 1)
                for place in range(2):
                    mine = group == (member + 2 * place) % GROUP
                    same[place] = jnp.where(mine, sum_same, same[place])
                    cross[place] = jnp.where(mine, sum_cross, cross[place])
            real = same[0] + swap_halves(same[1])
            imag = swap_halves(cross[1]) - cross[0]
            for part, value in enumerate((real, imag)):
                turn[later, half, part] = value
                out[quad, part, half] = jnp.concatenate(
                    [turn[later, half, part, pl.ds(low, 8, stride=2), :] for low in range(2)], axis=0
                ).astype(jnp.bfloat16)
        return carry

    lax.fori_loop(0, (quads + 1) // 2, visit, 0)


def hessian_kernel(meta, delta, weights_0, weights_1, sky_0, sky_1, tables, out):
    quads = (meta[5, 0] + GROUP - 1) // GROUP
    lane = lane_index(HALF_ROWS)
    right_forward, left_forward = tables[0], tables[1]
    right_inverse, left_inverse = tables[2], tables[3]
    wide = jnp.float32
    half_type = jnp.bfloat16
    channels = SETS * CH_DEV
    images = [(member, channel) for member in range(QUADS_STEP) for channel in range(channels)]

    def weight(quad, channel):
        return (weights_0, weights_1)[channel // CH_DEV][quad, channel % CH_DEV]

    def bright(quad, channel):
        return (sky_0, sky_1)[channel // CH_DEV][quad, channel % CH_DEV]

    def dot(a, b):
        return jnp.dot(a, b, preferred_element_type=wide)

    def to_rows(value):
        groups = []
        for group in range(len(images) // GROUP):
            pieces = []
            for member in range(GROUP):
                first = (group * GROUP + member) * W
                for part in range(2):
                    pieces.append(value[first : first + W, part * LANES : (part + 1) * LANES])
            groups.append(jnp.concatenate(pieces, axis=0))
        return jnp.concatenate(groups, axis=1)

    def piece(value, image, part):
        group, member = image // GROUP, image % GROUP
        first = (member * 2 + part) * W
        return value[first : first + W, group * LANES : (group + 1) * LANES]

    def both_parts(make):
        return jnp.concatenate(
            [
                jnp.concatenate([make(image, part) for part in range(2)], axis=1)
                for image in range(len(images))
            ],
            axis=0,
        )

    def visit(step, carry):
        quad_of = [step * QUADS_STEP + member for member in range(QUADS_STEP)]
        odd = []
        for quad in quad_of:
            value = jnp.full((HALF_ROWS, LANES), meta[7, quad * GROUP], jnp.int32)
            for member in range(1, GROUP):
                value = jnp.where(lane >= member * W, meta[7, quad * GROUP + member], value)
            odd.append(value > 0)

        def both_rows(member, part):
            first, second = (
                delta[quad_of[member], part, half].astype(wide) for half in range(HALVES)
            )
            rows = [
                jnp.where(odd[member], second, first),
                jnp.where(odd[member], first, second),
            ]
            return jnp.concatenate(rows, axis=0).astype(half_type)

        fields = [
            [both_rows(member, part) for part in range(2)] for member in range(QUADS_STEP)
        ]

        def lift(image, part):
            member, channel = images[image]
            return bright(quad_of[member], channel) * fields[member][part]

        middle = dot(both_parts(lift), right_forward).astype(half_type)
        freq = dot(left_forward, to_rows(middle))

        def weigh(image, part):
            member, channel = images[image]
            factor = weight(quad_of[member], channel).astype(wide)
            return (piece(freq, image, part) * factor).astype(half_type)

        middle = dot(both_parts(weigh), right_inverse).astype(half_type)
        back = dot(left_inverse, to_rows(middle))
        for member, quad in enumerate(quad_of):
            for part in range(2):
                total = None
                for channel in range(channels):
                    term = bright(quad, channel).astype(wide) * piece(
                        back, images.index((member, channel)), part
                    )
                    total = term if total is None else total + term
                even_rows, odd_rows = total[:HALF_ROWS], total[HALF_ROWS:]
                chunks = (
                    jnp.where(odd[member], odd_rows, even_rows),
                    jnp.where(odd[member], even_rows, odd_rows),
                )
                for half in range(HALVES):
                    out[quad, part, half] = chunks[half].astype(half_type)
        return carry

    lax.fori_loop(0, (quads + QUADS_STEP - 1) // QUADS_STEP, visit, 0)


def product_kernel(
    channels_total,
    meta,
    kept,
    over_two,
    beams,
    turned,
    out_own,
    out_chips,
    out_sibling,
    totals_p0,
    totals_p1,
    totals_q0,
    totals_q1,
    turn,
):
    live = meta[5, 0]
    quads = (live + GROUP - 1) // GROUP
    totals_p, totals_q = (totals_p0, totals_p1), (totals_q0, totals_q1)
    for totals in totals_p + totals_q:
        totals[...] = jnp.zeros_like(totals)
    group = group_index(HALF_ROWS)
    scale = 1.0 / channels_total

    def visit(quad, carry):
        for half in range(HALVES):
            for part in range(2):
                total = kept[quad, part, half].astype(jnp.float32)
                total = total + over_two[quad, part, half].astype(jnp.float32)
                total = total * scale
                for low in range(2):
                    turn[half, part, pl.ds(low, 8, stride=2), :] = total[low * 8 : (low + 1) * 8]
        for half in range(HALVES):
            real, imag = turn[half, 0], turn[half, 1]
            real_high, imag_high = swap_halves(real), swap_halves(imag)
            for member in range(GROUP):
                slot = quad * GROUP + member
                rows = pl.ds(meta[(2, 4)[half], slot], HALF_ROWS)
                station_p, station_q = meta[0, slot], meta[1, slot]
                shift = lax.rem(meta[3, slot] + 2 * G - member * W, 2 * G)
                alive = slot < live
                low = (group == member) & alive
                high = (group == (member + 2) % GROUP) & alive
                grad_real = jnp.where(low, real, jnp.where(high, real_high, 0.0))
                grad_imag = jnp.where(low, -imag, jnp.where(high, imag_high, 0.0))
                grad_real = pltpu.roll(grad_real, shift, 1)
                grad_imag = pltpu.roll(grad_imag, shift, 1)
                totals_p[half][station_p, rows, :] += (
                    beams[station_q, half, rows, :] * grad_real
                    + turned[station_q, half, rows, :] * grad_imag
                )
                totals_q[half][station_q, rows, :] += (
                    beams[station_p, half, rows, :] * grad_real
                    - turned[station_p, half, rows, :] * grad_imag
                )
        return carry

    lax.fori_loop(0, quads, visit, 0)

    def total(block, half):
        stations = pl.ds(block * ST_DEV, ST_DEV)
        return totals_p[half][stations] + totals_q[half][stations]

    for half in range(HALVES):
        out_own[:, half] = total(0, half)
        for block in range(2):
            out_chips[block, :, half] = total(1 + block, half)
            out_sibling[block, :, half] = total(3 + block, half).astype(jnp.bfloat16)


def result_kernel(mine, over_two, over_one, out, stage):
    chan = lax.axis_index("chan")
    high, low = chan % 2, chan // 2 % 2
    lower = lane_index(G // 2) < G
    for turn, value in enumerate((mine, over_two, over_one.at[0], over_one.at[1])):
        pol = (high ^ (turn // 2)) * 2 + (low ^ (turn % 2))
        for station in range(ST_DEV):
            even = value[station, 0].astype(jnp.float32)
            odd = value[station, 1].astype(jnp.float32)
            real = jnp.where(lower, even, swap_halves(odd))
            imag = jnp.where(lower, swap_halves(even), odd)
            stage[station, pl.ds(pol, G // 2, stride=2 * POLS), :] = real
            stage[station, pl.ds(pol + POLS, G // 2, stride=2 * POLS), :] = imag
    for station in range(ST_DEV):
        for pair in range(G // 2):
            out[station, :, pair * 2 * G : (pair + 1) * 2 * G] = stage[
                station, pair * 2 * POLS : (pair + 1) * 2 * POLS, :
            ]


def call(kernel, out_shape, in_specs, scratch_shapes, mebibytes=20):
    return pl.pallas_call(
        kernel,
        out_shape=out_shape,
        in_specs=in_specs,
        out_specs=jax.tree.map(lambda _: pl.BlockSpec(memory_space=VMEM), out_shape),
        scratch_shapes=scratch_shapes,
        compiler_params=pltpu.CompilerParams(vmem_limit_bytes=mebibytes * 1024 * 1024),
    )


def per_device(screens, direction, sky, weights, pairs, pointing, counts):
    base_count = lax.axis_size("base")
    myself = lax.axis_index("base")
    channels_total = CH_DEV * lax.axis_size("chan")
    core, chip_odd = myself % 2, myself // 2 % 2
    in_smem = pl.BlockSpec(memory_space=SMEM)
    in_vmem = pl.BlockSpec(memory_space=VMEM)

    own = call(
        own_kernel,
        jax.ShapeDtypeStruct((ST_DEV, 2, HALVES, G // 2, 2 * G), jnp.bfloat16),
        [in_vmem] * 2,
        [pltpu.VMEM((2 * ST_DEV, G * POLS, 2 * G), jnp.float32)],
    )(screens, direction)
    chip_a = across_chips(own, 0)
    meta = call(
        slots_kernel,
        jax.ShapeDtypeStruct((8, SUB_DEV), jnp.int32),
        [in_vmem] * 2 + [in_smem],
        [],
    )(pairs.T, pointing[None], counts)
    chip_b = across_chips(own, 1)
    weights_sent, sky_sent, meta = lax.optimization_barrier((weights, sky, meta))
    other = across_chan(jnp.concatenate([weights_sent, sky_sent]), 1)
    meta, chip_a, chip_b = lax.optimization_barrier((meta, chip_a, chip_b))
    shared_is_a = core == chip_odd
    sibling = to_sibling(jnp.stack([own, jnp.where(shared_is_a, chip_a, chip_b)]))

    delta_shape = (QUADS, 2, HALVES, HALF_ROWS, LANES)
    turn = pltpu.VMEM((HALVES, 2, HALF_ROWS, LANES), jnp.float32)
    field_shape = (NEAR * ST_DEV, HALVES, G // 2, 2 * G)
    field = pltpu.VMEM(field_shape, jnp.float32)
    delta, beams, turned = call(
        delta_kernel,
        [jax.ShapeDtypeStruct(delta_shape, jnp.bfloat16)]
        + [jax.ShapeDtypeStruct(field_shape, jnp.float32)] * 2,
        [in_smem] + [in_vmem] * 4,
        [field, pltpu.VMEM((2, HALVES, 2, HALF_ROWS, LANES), jnp.float32)],
    )(meta, own, chip_a, chip_b, sibling)
    over_two = across_chan(delta, 2)
    wide = jnp.float32
    tables = pass_tables()
    quad_shape = jax.ShapeDtypeStruct((QUADS, CH_DEV, W, LANES), jnp.bfloat16)

    mover = group_table()

    def prepared(weights, sky, first):
        return call(
            functools.partial(prepare_kernel, first),
            [quad_shape] * 2,
            [in_smem] + [in_vmem] * 3,
            [
                pltpu.VMEM((SUB_DEV, 8 * CH_DEV, LANES), wide),
                pltpu.VMEM((point_count, 8 * CH_DEV, LANES), wide),
            ],
        )(meta, weights, sky, mover)

    point_count = sky.shape[0]
    own_images = prepared(weights, sky, 0)
    other_images = prepared(other, other, SUB_DEV)
    weighting, brightness = zip(own_images, other_images)

    def hessian(delta):
        return call(
            hessian_kernel,
            jax.ShapeDtypeStruct(delta_shape, jnp.bfloat16),
            [in_smem] + [in_vmem] * 6,
            [],
            40,
        )(meta, delta, *weighting, *brightness, tables)

    sent, delta = lax.optimization_barrier((hessian(over_two), delta))
    back_two = across_chan(sent, 2)
    kept = hessian(delta)

    def make_product(*args):
        return product_kernel(channels_total, *args)

    block_shape = (ST_DEV, HALVES, G // 2, 2 * G)
    sum_own, sum_chips, sum_sibling = call(
        make_product,
        [
            jax.ShapeDtypeStruct(block_shape, wide),
            jax.ShapeDtypeStruct((2,) + block_shape, wide),
            jax.ShapeDtypeStruct((2,) + block_shape, jnp.bfloat16),
        ],
        [in_smem] + [in_vmem] * 4,
        [pltpu.VMEM((NEAR * ST_DEV, G // 2, 2 * G), wide)] * 4 + [turn],
    )(meta, kept, back_two, beams, turned)
    from_sibling = to_sibling(sum_sibling).astype(wide)
    sum_a = sum_chips[0] + jnp.where(shared_is_a, from_sibling[1], 0.0)
    sum_b = sum_chips[1] + jnp.where(shared_is_a, 0.0, from_sibling[1])
    from_b = across_chips(sum_b.astype(jnp.bfloat16), 1)
    from_a = across_chips(sum_a.astype(jnp.bfloat16), 0)
    mine = sum_own + from_sibling[0] + from_b.astype(wide) + from_a.astype(wide)
    mine = mine.astype(jnp.bfloat16)
    other = across_chan(mine, 4)
    mine = (mine.astype(wide) + other.astype(wide)).astype(jnp.bfloat16)
    over_two = across_chan(mine, 2)
    over_one = across_chan(jnp.stack([mine, over_two]), 1)
    return call(
        result_kernel,
        jax.ShapeDtypeStruct((ST_DEV, 2 * POLS, G * G), wide),
        [in_vmem] * 3,
        [pltpu.VMEM((ST_DEV, G // 2 * 2 * POLS, 2 * G), wide)],
    )(mine, over_two, over_one)


def solution(mesh):
    in_specs = (
        P("base", None, None),
        P("base", None, None),
        P(None, "chan", None),
        P("base", "chan", None),
        P("base", None),
        P("base"),
        P("base"),
    )
    out_specs = P("base", None, None)
    return jax.shard_map(
        per_device, mesh=mesh, in_specs=in_specs, out_specs=out_specs, check_vma=False
    )
```

```python
import functools
import math

import jax
import jax.numpy as jnp
import ml_dtypes
import numpy as np
from jax import lax
from jax.experimental import pallas as pl
from jax.experimental.pallas import tpu as pltpu
from jax.sharding import PartitionSpec as P

G = 64
W = 32
REACH = 2
ST_DEV = 4
SUB_DEV = 32
CH_DEV = 8
POLS = 4
HALVES = 2
GROUP = 4
QUADS = SUB_DEV // GROUP
HALF_ROWS = W // HALVES
PARTS = POLS * HALVES
LANES = GROUP * W
NEAR = 2 * REACH + 1
QUADS_STEP = 8
SETS = 2
SMEM = pltpu.SMEM
VMEM = pltpu.VMEM


def across_chan(value, bit):
    count = lax.axis_size("chan")
    return lax.ppermute(value, "chan", [(i, i ^ bit) for i in range(count)])


def to_sibling(value):
    count = lax.axis_size("base")
    return lax.ppermute(value, "base", [(i, i ^ 1) for i in range(count)])


def turned_half(base, base_count):
    return base * 2 // base_count


def across_chips(value, phase):
    base_count, chan_count = lax.axis_size("base"), lax.axis_size("chan")
    perm = []
    for chan in range(chan_count):
        for base in range(base_count):
            step = 2 if (base // 2 + phase) % 2 == 0 else -2
            target = (base + step) % base_count
            turn = turned_half(base, base_count) ^ turned_half(target, base_count)
            perm.append((chan * base_count + base, (chan ^ (4 * turn)) * base_count + target))
    return lax.ppermute(value, ("chan", "base"), perm)


def pass_tables():
    position = np.arange(W, dtype=np.int32)
    product = position[:, None] * position[None, :] % W
    angles = product.astype(np.float32) * np.float32(2.0 * math.pi / W)
    norm_factor = np.float32(1.0 / math.sqrt(W))
    cosine = np.cos(angles) * norm_factor
    sine = np.sin(angles) * norm_factor
    order = np.arange(W).reshape(8, 4).T[[0, 2, 1, 3]].reshape(W)
    cosine_rows, sine_rows = cosine[order][:, order], sine[order][:, order]
    eye = np.eye(GROUP, dtype=np.float32)

    def right(sign):
        cos_block, sin_block = np.kron(eye, cosine), sign * np.kron(eye, sine)
        return np.block([[cos_block, sin_block], [-sin_block, cos_block]])

    def left(sign):
        turn = np.block([[cosine_rows, -sign * sine_rows], [sign * sine_rows, cosine_rows]])
        return np.kron(eye, turn)

    tables = np.stack([right(-1.0), left(-1.0), right(1.0), left(1.0)])
    return jnp.asarray(tables.astype(ml_dtypes.bfloat16))


def swap_halves(value):
    return pltpu.roll(value, G, 1)


def lane_index(rows):
    return lax.broadcasted_iota(jnp.int32, (rows, 2 * G), 1)


def slots_kernel(pairs, pointing, counts, out):
    base_count = lax.axis_size("base")
    myself = lax.axis_index("base")
    core, chip_odd = lax.rem(myself, 2), lax.rem(myself // 2, 2)
    live = counts[0]
    slot = lax.broadcasted_iota(jnp.int32, (2, SUB_DEV), 1)
    station = pairs[...]
    offset = (station >> 2) - myself
    offset = jnp.where(offset > base_count // 2, offset - base_count, offset)
    offset = jnp.where(offset < -(base_count // 2), offset + base_count, offset)
    two_away = jnp.where((offset > 0) == (chip_odd == 0), 1, 2)
    one_away = jnp.where((offset > 0) == (core == 1), 4, 3)
    far = jnp.abs(offset) == 2
    block = jnp.where(offset == 0, 0, jnp.where(far, two_away, one_away))
    place = jnp.where(slot < live, block * ST_DEV + (station & (ST_DEV - 1)), 0)
    out[0:2, :] = place
    point = pointing[...]

    def start(index):
        value = jnp.zeros_like(index)
        for step in range(1, 4):
            value = jnp.where(index == step, step * (G - W) // 3, value)
        return value

    row = start(point >> 2)
    out[2:3, :] = (row + 1) >> 1
    out[3:4, :] = start(point & 3)
    out[4:5, :] = row >> 1
    out[5:6, :] = jnp.full((1, SUB_DEV), live, jnp.int32)
    out[6:7, :] = point
    out[7:8, :] = row & 1


def group_table():
    place = np.arange(GROUP * LANES).reshape(GROUP, GROUP, W).transpose(1, 0, 2).reshape(-1)
    return jnp.asarray(np.eye(GROUP * LANES)[:, place].astype(ml_dtypes.bfloat16))


def prepare_kernel(first, meta, weights, sky, table, weight_out, sky_out, stage, sky_stage):
    def store(value, dest):
        for high in range(8):
            dest[high * CH_DEV : (high + 1) * CH_DEV, :] = value[
                :, high * LANES : (high + 1) * LANES
            ]

    def side_by_side(stages):
        return jnp.concatenate(
            [
                jnp.concatenate(
                    [
                        stages(quad * GROUP + member)[pl.ds(channel, 8, stride=CH_DEV), :]
                        for member in range(GROUP)
                    ],
                    axis=1,
                )
                for quad in range(QUADS)
                for channel in range(CH_DEV)
            ],
            axis=0,
        ).astype(jnp.bfloat16)

    def write(moved, out):
        for quad in range(QUADS):
            for channel in range(CH_DEV):
                rows = (quad * CH_DEV + channel) * 8
                out[quad, channel] = jnp.concatenate(
                    [
                        moved[rows : rows + 8, low * LANES : (low + 1) * LANES]
                        for low in (0, 2, 1, 3)
                    ],
                    axis=0,
                ).astype(jnp.bfloat16)

    for slot in range(SUB_DEV):
        store(weights[slot].astype(jnp.float32), stage.at[slot])
    for point in range(sky_stage.shape[0]):
        store(sky[first + point].astype(jnp.float32), sky_stage.at[point])
    mover = table[...]
    moved = jnp.dot(
        side_by_side(lambda slot: stage.at[slot]), mover, preferred_element_type=jnp.float32
    )
    write(moved, weight_out)
    moved = jnp.dot(
        side_by_side(lambda slot: sky_stage.at[meta[6, slot]]),
        mover,
        preferred_element_type=jnp.float32,
    )
    write(moved, sky_out)


def own_kernel(screens, direction, out, stage):
    chan = lax.axis_index("chan")
    pol = chan % 2 * 2 + chan // 2 % 2
    lower = lane_index(G // 2) < G
    for station in range(ST_DEV):
        for kind, source in enumerate((screens, direction)):
            value = source[station].astype(jnp.float32)
            spot = stage.at[station * 2 + kind]
            for pair in range(G // 2):
                spot[pair * 2 * POLS : (pair + 1) * 2 * POLS, :] = value[
                    :, pair * 2 * G : (pair + 1) * 2 * G
                ]
            real = spot[pl.ds(pol, G // 2, stride=2 * POLS), :]
            imag = spot[pl.ds(pol + POLS, G // 2, stride=2 * POLS), :]
            even = jnp.where(lower, real, swap_halves(imag))
            odd = jnp.where(lower, swap_halves(real), imag)
            out[station, kind, 0] = even.astype(jnp.bfloat16)
            out[station, kind, 1] = odd.astype(jnp.bfloat16)


def group_index(rows):
    return lane_index(rows) // W


def delta_kernel(
    meta, own, chip_a, chip_b, sibling, out, beams, turned, probes, turn
):
    quads = (meta[5, 0] + GROUP - 1) // GROUP
    for block, value in enumerate((own, chip_a, chip_b, sibling.at[0], sibling.at[1])):
        for member in range(ST_DEV):
            station = block * ST_DEV + member
            for half in range(HALVES):
                beam = value[member, 0, half].astype(jnp.float32)
                beams[station, half] = beam
                probes[station, half] = value[member, 1, half].astype(jnp.float32)
                turned[station, half] = swap_halves(beam)
    group = group_index(HALF_ROWS)

    def visit(step, carry):
        for half, later in [(half, later) for half in range(HALVES) for later in range(2)]:
            quad = 2 * step + later
            same = [jnp.zeros((HALF_ROWS, LANES), jnp.float32)] * 2
            cross = [jnp.zeros((HALF_ROWS, LANES), jnp.float32)] * 2
            for member in range(GROUP):
                slot = quad * GROUP + member
                rows = pl.ds(meta[(2, 4)[half], slot], HALF_ROWS)
                station_p, station_q = meta[0, slot], meta[1, slot]
                probe_p = probes[station_p, half, rows, :]
                probe_q = probes[station_q, half, rows, :]
                beam_p = beams[station_p, half, rows, :]
                beam_q = beams[station_q, half, rows, :]
                sum_same = probe_p * beam_q + beam_p * probe_q
                sum_cross = (
                    probe_p * turned[station_q, half, rows, :]
                    - turned[station_p, half, rows, :] * probe_q
                )
                shift = lax.rem(member * W + 2 * G - meta[3, slot], 2 * G)
                sum_same = pltpu.roll(sum_same, shift, 1)
                sum_cross = pltpu.roll(sum_cross, shift, 1)
                for place in range(2):
                    mine = group == (member + 2 * place) % GROUP
                    same[place] = jnp.where(mine, sum_same, same[place])
                    cross[place] = jnp.where(mine, sum_cross, cross[place])
            real = same[0] + swap_halves(same[1])
            imag = swap_halves(cross[1]) - cross[0]
            for part, value in enumerate((real, imag)):
                turn[later, half, part] = value
                out[quad, part, half] = jnp.concatenate(
                    [turn[later, half, part, pl.ds(low, 8, stride=2), :] for low in range(2)], axis=0
                ).astype(jnp.bfloat16)
        return carry

    lax.fori_loop(0, (quads + 1) // 2, visit, 0)


def hessian_kernel(meta, delta, weights_0, weights_1, sky_0, sky_1, tables, out):
    quads = (meta[5, 0] + GROUP - 1) // GROUP
    lane = lane_index(HALF_ROWS)
    right_forward, left_forward = tables[0], tables[1]
    right_inverse, left_inverse = tables[2], tables[3]
    wide = jnp.float32
    half_type = jnp.bfloat16
    channels = SETS * CH_DEV
    images = [(member, channel) for member in range(QUADS_STEP) for channel in range(channels)]

    def weight(quad, channel):
        return (weights_0, weights_1)[channel // CH_DEV][quad, channel % CH_DEV]

    def bright(quad, channel):
        return (sky_0, sky_1)[channel // CH_DEV][quad, channel % CH_DEV]

    def dot(a, b):
        return jnp.dot(a, b, preferred_element_type=wide)

    def to_rows(value):
        groups = []
        for group in range(len(images) // GROUP):
            pieces = []
            for member in range(GROUP):
                first = (group * GROUP + member) * W
                for part in range(2):
                    pieces.append(value[first : first + W, part * LANES : (part + 1) * LANES])
            groups.append(jnp.concatenate(pieces, axis=0))
        return jnp.concatenate(groups, axis=1)

    def piece(value, image, part):
        group, member = image // GROUP, image % GROUP
        first = (member * 2 + part) * W
        return value[first : first + W, group * LANES : (group + 1) * LANES]

    def both_parts(make):
        return jnp.concatenate(
            [
                jnp.concatenate([make(image, part) for part in range(2)], axis=1)
                for image in range(len(images))
            ],
            axis=0,
        )

    def visit(step, carry):
        quad_of = [step * QUADS_STEP + member for member in range(QUADS_STEP)]
        odd = []
        for quad in quad_of:
            value = jnp.full((HALF_ROWS, LANES), meta[7, quad * GROUP], jnp.int32)
            for member in range(1, GROUP):
                value = jnp.where(lane >= member * W, meta[7, quad * GROUP + member], value)
            odd.append(value > 0)

        def both_rows(member, part):
            first, second = (
                delta[quad_of[member], part, half].astype(wide) for half in range(HALVES)
            )
            rows = [
                jnp.where(odd[member], second, first),
                jnp.where(odd[member], first, second),
            ]
            return jnp.concatenate(rows, axis=0).astype(half_type)

        fields = [
            [both_rows(member, part) for part in range(2)] for member in range(QUADS_STEP)
        ]

        def lift(image, part):
            member, channel = images[image]
            return bright(quad_of[member], channel) * fields[member][part]

        middle = dot(both_parts(lift), right_forward).astype(half_type)
        freq = dot(left_forward, to_rows(middle))

        def weigh(image, part):
            member, channel = images[image]
            factor = weight(quad_of[member], channel).astype(wide)
            return (piece(freq, image, part) * factor).astype(half_type)

        middle = dot(both_parts(weigh), right_inverse).astype(half_type)
        back = dot(left_inverse, to_rows(middle))
        for member, quad in enumerate(quad_of):
            for part in range(2):
                total = None
                for channel in range(channels):
                    term = bright(quad, channel).astype(wide) * piece(
                        back, images.index((member, channel)), part
                    )
                    total = term if total is None else total + term
                even_rows, odd_rows = total[:HALF_ROWS], total[HALF_ROWS:]
                chunks = (
                    jnp.where(odd[member], odd_rows, even_rows),
                    jnp.where(odd[member], even_rows, odd_rows),
                )
                for half in range(HALVES):
                    out[quad, part, half] = chunks[half].astype(half_type)
        return carry

    lax.fori_loop(0, (quads + QUADS_STEP - 1) // QUADS_STEP, visit, 0)


def product_kernel(
    channels_total,
    meta,
    kept,
    over_two,
    beams,
    turned,
    out_own,
    out_chips,
    out_sibling,
    totals_p0,
    totals_p1,
    totals_q0,
    totals_q1,
    turn,
):
    live = meta[5, 0]
    quads = (live + GROUP - 1) // GROUP
    totals_p, totals_q = (totals_p0, totals_p1), (totals_q0, totals_q1)
    for totals in totals_p + totals_q:
        totals[...] = jnp.zeros_like(totals)
    group = group_index(HALF_ROWS)
    scale = 1.0 / channels_total

    def visit(quad, carry):
        for half in range(HALVES):
            for part in range(2):
                total = kept[quad, part, half].astype(jnp.float32)
                total = total + over_two[quad, part, half].astype(jnp.float32)
                total = total * scale
                for low in range(2):
                    turn[half, part, pl.ds(low, 8, stride=2), :] = total[low * 8 : (low + 1) * 8]
        for half in range(HALVES):
            real, imag = turn[half, 0], turn[half, 1]
            real_high, imag_high = swap_halves(real), swap_halves(imag)
            for member in range(GROUP):
                slot = quad * GROUP + member
                rows = pl.ds(meta[(2, 4)[half], slot], HALF_ROWS)
                station_p, station_q = meta[0, slot], meta[1, slot]
                shift = lax.rem(meta[3, slot] + 2 * G - member * W, 2 * G)
                alive = slot < live
                low = (group == member) & alive
                high = (group == (member + 2) % GROUP) & alive
                grad_real = jnp.where(low, real, jnp.where(high, real_high, 0.0))
                grad_imag = jnp.where(low, -imag, jnp.where(high, imag_high, 0.0))
                grad_real = pltpu.roll(grad_real, shift, 1)
                grad_imag = pltpu.roll(grad_imag, shift, 1)
                totals_p[half][station_p, rows, :] += (
                    beams[station_q, half, rows, :] * grad_real
                    + turned[station_q, half, rows, :] * grad_imag
                )
                totals_q[half][station_q, rows, :] += (
                    beams[station_p, half, rows, :] * grad_real
                    - turned[station_p, half, rows, :] * grad_imag
                )
        return carry

    lax.fori_loop(0, quads, visit, 0)

    def total(block, half):
        stations = pl.ds(block * ST_DEV, ST_DEV)
        return totals_p[half][stations] + totals_q[half][stations]

    for half in range(HALVES):
        out_own[:, half] = total(0, half)
        for block in range(2):
            out_chips[block, :, half] = total(1 + block, half)
            out_sibling[block, :, half] = total(3 + block, half).astype(jnp.bfloat16)


def result_kernel(mine, over_two, over_one, out, stage):
    chan = lax.axis_index("chan")
    high, low = chan % 2, chan // 2 % 2
    lower = lane_index(G // 2) < G
    for turn, value in enumerate((mine, over_two, over_one.at[0], over_one.at[1])):
        pol = (high ^ (turn // 2)) * 2 + (low ^ (turn % 2))
        for station in range(ST_DEV):
            even = value[station, 0].astype(jnp.float32)
            odd = value[station, 1].astype(jnp.float32)
            real = jnp.where(lower, even, swap_halves(odd))
            imag = jnp.where(lower, swap_halves(even), odd)
            stage[station, pl.ds(pol, G // 2, stride=2 * POLS), :] = real
            stage[station, pl.ds(pol + POLS, G // 2, stride=2 * POLS), :] = imag
    for station in range(ST_DEV):
        for pair in range(G // 2):
            out[station, :, pair * 2 * G : (pair + 1) * 2 * G] = stage[
                station, pair * 2 * POLS : (pair + 1) * 2 * POLS, :
            ]


def call(kernel, out_shape, in_specs, scratch_shapes, mebibytes=20):
    return pl.pallas_call(
        kernel,
        out_shape=out_shape,
        in_specs=in_specs,
        out_specs=jax.tree.map(lambda _: pl.BlockSpec(memory_space=VMEM), out_shape),
        scratch_shapes=scratch_shapes,
        compiler_params=pltpu.CompilerParams(vmem_limit_bytes=mebibytes * 1024 * 1024),
    )


def per_device(screens, direction, sky, weights, pairs, pointing, counts):
    base_count = lax.axis_size("base")
    myself = lax.axis_index("base")
    channels_total = CH_DEV * lax.axis_size("chan")
    core, chip_odd = myself % 2, myself // 2 % 2
    in_smem = pl.BlockSpec(memory_space=SMEM)
    in_vmem = pl.BlockSpec(memory_space=VMEM)

    both = jnp.concatenate([weights, sky])
    both, screens, direction = lax.optimization_barrier((both, screens, direction))
    own = call(
        own_kernel,
        jax.ShapeDtypeStruct((ST_DEV, 2, HALVES, G // 2, 2 * G), jnp.bfloat16),
        [in_vmem] * 2,
        [pltpu.VMEM((2 * ST_DEV, G * POLS, 2 * G), jnp.float32)],
    )(screens, direction)
    chip_a = across_chips(own, 0)
    meta = call(
        slots_kernel,
        jax.ShapeDtypeStruct((8, SUB_DEV), jnp.int32),
        [in_vmem] * 2 + [in_smem],
        [],
    )(pairs.T, pointing[None], counts)
    chip_b = across_chips(own, 1)
    both, meta = lax.optimization_barrier((both, meta))
    other = across_chan(both, 1)
    meta, chip_a, chip_b = lax.optimization_barrier((meta, chip_a, chip_b))
    shared_is_a = core == chip_odd
    sibling = to_sibling(jnp.stack([own, jnp.where(shared_is_a, chip_a, chip_b)]))

    delta_shape = (QUADS, 2, HALVES, HALF_ROWS, LANES)
    turn = pltpu.VMEM((HALVES, 2, HALF_ROWS, LANES), jnp.float32)
    field_shape = (NEAR * ST_DEV, HALVES, G // 2, 2 * G)
    field = pltpu.VMEM(field_shape, jnp.float32)
    delta, beams, turned = call(
        delta_kernel,
        [jax.ShapeDtypeStruct(delta_shape, jnp.bfloat16)]
        + [jax.ShapeDtypeStruct(field_shape, jnp.float32)] * 2,
        [in_smem] + [in_vmem] * 4,
        [field, pltpu.VMEM((2, HALVES, 2, HALF_ROWS, LANES), jnp.float32)],
    )(meta, own, chip_a, chip_b, sibling)
    over_two = across_chan(delta, 2)
    wide = jnp.float32
    tables = pass_tables()
    quad_shape = jax.ShapeDtypeStruct((QUADS, CH_DEV, W, LANES), jnp.bfloat16)

    mover = group_table()

    def prepared(weights, sky, first):
        return call(
            functools.partial(prepare_kernel, first),
            [quad_shape] * 2,
            [in_smem] + [in_vmem] * 3,
            [
                pltpu.VMEM((SUB_DEV, 8 * CH_DEV, LANES), wide),
                pltpu.VMEM((point_count, 8 * CH_DEV, LANES), wide),
            ],
        )(meta, weights, sky, mover)

    point_count = sky.shape[0]
    own_images = prepared(weights, sky, 0)
    other_images = prepared(other, other, SUB_DEV)
    weighting, brightness = zip(own_images, other_images)

    def hessian(delta):
        return call(
            hessian_kernel,
            jax.ShapeDtypeStruct(delta_shape, jnp.bfloat16),
            [in_smem] + [in_vmem] * 6,
            [],
            40,
        )(meta, delta, *weighting, *brightness, tables)

    sent, delta = lax.optimization_barrier((hessian(over_two), delta))
    back_two = across_chan(sent, 2)
    kept = hessian(delta)

    def make_product(*args):
        return product_kernel(channels_total, *args)

    block_shape = (ST_DEV, HALVES, G // 2, 2 * G)
    sum_own, sum_chips, sum_sibling = call(
        make_product,
        [
            jax.ShapeDtypeStruct(block_shape, wide),
            jax.ShapeDtypeStruct((2,) + block_shape, wide),
            jax.ShapeDtypeStruct((2,) + block_shape, jnp.bfloat16),
        ],
        [in_smem] + [in_vmem] * 4,
        [pltpu.VMEM((NEAR * ST_DEV, G // 2, 2 * G), wide)] * 4 + [turn],
    )(meta, kept, back_two, beams, turned)
    from_sibling = to_sibling(sum_sibling).astype(wide)
    sum_a = sum_chips[0] + jnp.where(shared_is_a, from_sibling[1], 0.0)
    sum_b = sum_chips[1] + jnp.where(shared_is_a, 0.0, from_sibling[1])
    from_b = across_chips(sum_b.astype(jnp.bfloat16), 1)
    from_a = across_chips(sum_a.astype(jnp.bfloat16), 0)
    mine = sum_own + from_sibling[0] + from_b.astype(wide) + from_a.astype(wide)
    mine = mine.astype(jnp.bfloat16)
    other = across_chan(mine, 4)
    mine = (mine.astype(wide) + other.astype(wide)).astype(jnp.bfloat16)
    over_two = across_chan(mine, 2)
    over_one = across_chan(jnp.stack([mine, over_two]), 1)
    return call(
        result_kernel,
        jax.ShapeDtypeStruct((ST_DEV, 2 * POLS, G * G), wide),
        [in_vmem] * 3,
        [pltpu.VMEM((ST_DEV, G // 2 * 2 * POLS, 2 * G), wide)],
    )(mine, over_two, over_one)


def solution(mesh):
    in_specs = (
        P("base", None, None),
        P("base", None, None),
        P(None, "chan", None),
        P("base", "chan", None),
        P("base", None),
        P("base"),
        P("base"),
    )
    out_specs = P("base", None, None)
    return jax.shard_map(
        per_device, mesh=mesh, in_specs=in_specs, out_specs=out_specs, check_vma=False
    )
```

```python
import functools
import math

import jax
import jax.numpy as jnp
import ml_dtypes
import numpy as np
from jax import lax
from jax.experimental import pallas as pl
from jax.experimental.pallas import tpu as pltpu
from jax.sharding import PartitionSpec as P

G = 64
W = 32
REACH = 2
ST_DEV = 4
SUB_DEV = 32
CH_DEV = 8
POLS = 4
HALVES = 2
GROUP = 4
QUADS = SUB_DEV // GROUP
HALF_ROWS = W // HALVES
PARTS = POLS * HALVES
LANES = GROUP * W
NEAR = 2 * REACH + 1
QUADS_STEP = 8
SETS = 2
SMEM = pltpu.SMEM
VMEM = pltpu.VMEM


def across_chan(value, bit):
    count = lax.axis_size("chan")
    return lax.ppermute(value, "chan", [(i, i ^ bit) for i in range(count)])


def to_sibling(value):
    count = lax.axis_size("base")
    return lax.ppermute(value, "base", [(i, i ^ 1) for i in range(count)])


def turned_half(base, base_count):
    return base * 2 // base_count


def across_chips(value, phase):
    base_count, chan_count = lax.axis_size("base"), lax.axis_size("chan")
    perm = []
    for chan in range(chan_count):
        for base in range(base_count):
            step = 2 if (base // 2 + phase) % 2 == 0 else -2
            target = (base + step) % base_count
            turn = turned_half(base, base_count) ^ turned_half(target, base_count)
            perm.append((chan * base_count + base, (chan ^ (4 * turn)) * base_count + target))
    return lax.ppermute(value, ("chan", "base"), perm)


def pass_tables():
    position = np.arange(W, dtype=np.int32)
    product = position[:, None] * position[None, :] % W
    angles = product.astype(np.float32) * np.float32(2.0 * math.pi / W)
    norm_factor = np.float32(1.0 / math.sqrt(W))
    cosine = np.cos(angles) * norm_factor
    sine = np.sin(angles) * norm_factor
    order = np.arange(W).reshape(8, 4).T[[0, 2, 1, 3]].reshape(W)
    cosine_rows, sine_rows = cosine[order][:, order], sine[order][:, order]
    eye = np.eye(GROUP, dtype=np.float32)

    def right(sign):
        cos_block, sin_block = np.kron(eye, cosine), sign * np.kron(eye, sine)
        return np.block([[cos_block, sin_block], [-sin_block, cos_block]])

    def left(sign):
        turn = np.block([[cosine_rows, -sign * sine_rows], [sign * sine_rows, cosine_rows]])
        return np.kron(eye, turn)

    tables = np.stack([right(-1.0), left(-1.0), right(1.0), left(1.0)])
    return jnp.asarray(tables.astype(ml_dtypes.bfloat16))


def swap_halves(value):
    return pltpu.roll(value, G, 1)


def lane_index(rows):
    return lax.broadcasted_iota(jnp.int32, (rows, 2 * G), 1)


def slots_kernel(pairs, pointing, counts, out):
    base_count = lax.axis_size("base")
    myself = lax.axis_index("base")
    core, chip_odd = lax.rem(myself, 2), lax.rem(myself // 2, 2)
    live = counts[0]
    slot = lax.broadcasted_iota(jnp.int32, (2, SUB_DEV), 1)
    station = pairs[...]
    offset = (station >> 2) - myself
    offset = jnp.where(offset > base_count // 2, offset - base_count, offset)
    offset = jnp.where(offset < -(base_count // 2), offset + base_count, offset)
    two_away = jnp.where((offset > 0) == (chip_odd == 0), 1, 2)
    one_away = jnp.where((offset > 0) == (core == 1), 4, 3)
    far = jnp.abs(offset) == 2
    block = jnp.where(offset == 0, 0, jnp.where(far, two_away, one_away))
    place = jnp.where(slot < live, block * ST_DEV + (station & (ST_DEV - 1)), 0)
    out[0:2, :] = place
    point = pointing[...]

    def start(index):
        value = jnp.zeros_like(index)
        for step in range(1, 4):
            value = jnp.where(index == step, step * (G - W) // 3, value)
        return value

    row = start(point >> 2)
    out[2:3, :] = (row + 1) >> 1
    out[3:4, :] = start(point & 3)
    out[4:5, :] = row >> 1
    out[5:6, :] = jnp.full((1, SUB_DEV), live, jnp.int32)
    out[6:7, :] = point
    out[7:8, :] = row & 1


def group_table():
    place = np.arange(GROUP * LANES).reshape(GROUP, GROUP, W).transpose(1, 0, 2).reshape(-1)
    return jnp.asarray(np.eye(GROUP * LANES)[:, place].astype(ml_dtypes.bfloat16))


def prepare_kernel(first, meta, weights, sky, table, weight_out, sky_out, stage, sky_stage):
    def store(value, dest):
        for high in range(8):
            dest[high * CH_DEV : (high + 1) * CH_DEV, :] = value[
                :, high * LANES : (high + 1) * LANES
            ]

    def side_by_side(stages):
        return jnp.concatenate(
            [
                jnp.concatenate(
                    [
                        stages(quad * GROUP + member)[pl.ds(channel, 8, stride=CH_DEV), :]
                        for member in range(GROUP)
                    ],
                    axis=1,
                )
                for quad in range(QUADS)
                for channel in range(CH_DEV)
            ],
            axis=0,
        ).astype(jnp.bfloat16)

    def write(moved, out):
        for quad in range(QUADS):
            for channel in range(CH_DEV):
                rows = (quad * CH_DEV + channel) * 8
                out[quad, channel] = jnp.concatenate(
                    [
                        moved[rows : rows + 8, low * LANES : (low + 1) * LANES]
                        for low in (0, 2, 1, 3)
                    ],
                    axis=0,
                ).astype(jnp.bfloat16)

    for slot in range(SUB_DEV):
        store(weights[slot].astype(jnp.float32), stage.at[slot])
    for point in range(sky_stage.shape[0]):
        store(sky[first + point].astype(jnp.float32), sky_stage.at[point])
    mover = table[...]
    moved = jnp.dot(
        side_by_side(lambda slot: stage.at[slot]), mover, preferred_element_type=jnp.float32
    )
    write(moved, weight_out)
    moved = jnp.dot(
        side_by_side(lambda slot: sky_stage.at[meta[6, slot]]),
        mover,
        preferred_element_type=jnp.float32,
    )
    write(moved, sky_out)


def own_kernel(screens, direction, out, stage):
    chan = lax.axis_index("chan")
    pol = chan % 2 * 2 + chan // 2 % 2
    lower = lane_index(G // 2) < G
    for station in range(ST_DEV):
        for kind, source in enumerate((screens, direction)):
            value = source[station].astype(jnp.float32)
            spot = stage.at[station * 2 + kind]
            for pair in range(G // 2):
                spot[pair * 2 * POLS : (pair + 1) * 2 * POLS, :] = value[
                    :, pair * 2 * G : (pair + 1) * 2 * G
                ]
            real = spot[pl.ds(pol, G // 2, stride=2 * POLS), :]
            imag = spot[pl.ds(pol + POLS, G // 2, stride=2 * POLS), :]
            even = jnp.where(lower, real, swap_halves(imag))
            odd = jnp.where(lower, swap_halves(real), imag)
            out[station, kind, 0] = even.astype(jnp.bfloat16)
            out[station, kind, 1] = odd.astype(jnp.bfloat16)


def group_index(rows):
    return lane_index(rows) // W


def delta_kernel(
    meta, own, chip_a, chip_b, sibling, out, beams, turned, probes, turn
):
    quads = (meta[5, 0] + GROUP - 1) // GROUP
    for block, value in enumerate((own, chip_a, chip_b, sibling.at[0], sibling.at[1])):
        for member in range(ST_DEV):
            station = block * ST_DEV + member
            for half in range(HALVES):
                beam = value[member, 0, half].astype(jnp.float32)
                beams[station, half] = beam
                probes[station, half] = value[member, 1, half].astype(jnp.float32)
                turned[station, half] = swap_halves(beam)
    group = group_index(HALF_ROWS)

    def visit(step, carry):
        for half, later in [(half, later) for half in range(HALVES) for later in range(2)]:
            quad = 2 * step + later
            same = [jnp.zeros((HALF_ROWS, LANES), jnp.float32)] * 2
            cross = [jnp.zeros((HALF_ROWS, LANES), jnp.float32)] * 2
            for member in range(GROUP):
                slot = quad * GROUP + member
                rows = pl.ds(meta[(2, 4)[half], slot], HALF_ROWS)
                station_p, station_q = meta[0, slot], meta[1, slot]
                probe_p = probes[station_p, half, rows, :]
                probe_q = probes[station_q, half, rows, :]
                beam_p = beams[station_p, half, rows, :]
                beam_q = beams[station_q, half, rows, :]
                sum_same = probe_p * beam_q + beam_p * probe_q
                sum_cross = (
                    probe_p * turned[station_q, half, rows, :]
                    - turned[station_p, half, rows, :] * probe_q
                )
                shift = lax.rem(member * W + 2 * G - meta[3, slot], 2 * G)
                sum_same = pltpu.roll(sum_same, shift, 1)
                sum_cross = pltpu.roll(sum_cross, shift, 1)
                for place in range(2):
                    mine = group == (member + 2 * place) % GROUP
                    same[place] = jnp.where(mine, sum_same, same[place])
                    cross[place] = jnp.where(mine, sum_cross, cross[place])
            real = same[0] + swap_halves(same[1])
            imag = swap_halves(cross[1]) - cross[0]
            for part, value in enumerate((real, imag)):
                turn[later, half, part] = value
                out[quad, part, half] = jnp.concatenate(
                    [turn[later, half, part, pl.ds(low, 8, stride=2), :] for low in range(2)], axis=0
                ).astype(jnp.bfloat16)
        return carry

    lax.fori_loop(0, (quads + 1) // 2, visit, 0)


def hessian_kernel(meta, delta, weights_0, weights_1, sky_0, sky_1, tables, out):
    quads = (meta[5, 0] + GROUP - 1) // GROUP
    lane = lane_index(HALF_ROWS)
    right_forward, left_forward = tables[0], tables[1]
    right_inverse, left_inverse = tables[2], tables[3]
    wide = jnp.float32
    half_type = jnp.bfloat16
    channels = SETS * CH_DEV
    images = [(member, channel) for member in range(QUADS_STEP) for channel in range(channels)]

    def weight(quad, channel):
        return (weights_0, weights_1)[channel // CH_DEV][quad, channel % CH_DEV]

    def bright(quad, channel):
        return (sky_0, sky_1)[channel // CH_DEV][quad, channel % CH_DEV]

    def dot(a, b):
        return jnp.dot(a, b, preferred_element_type=wide)

    def to_rows(value):
        groups = []
        for group in range(len(images) // GROUP):
            pieces = []
            for member in range(GROUP):
                first = (group * GROUP + member) * W
                for part in range(2):
                    pieces.append(value[first : first + W, part * LANES : (part + 1) * LANES])
            groups.append(jnp.concatenate(pieces, axis=0))
        return jnp.concatenate(groups, axis=1)

    def piece(value, image, part):
        group, member = image // GROUP, image % GROUP
        first = (member * 2 + part) * W
        return value[first : first + W, group * LANES : (group + 1) * LANES]

    def both_parts(make):
        return jnp.concatenate(
            [
                jnp.concatenate([make(image, part) for part in range(2)], axis=1)
                for image in range(len(images))
            ],
            axis=0,
        )

    def visit(step, carry):
        quad_of = [step * QUADS_STEP + member for member in range(QUADS_STEP)]
        odd = []
        for quad in quad_of:
            value = jnp.full((HALF_ROWS, LANES), meta[7, quad * GROUP], jnp.int32)
            for member in range(1, GROUP):
                value = jnp.where(lane >= member * W, meta[7, quad * GROUP + member], value)
            odd.append(value > 0)

        def both_rows(member, part):
            first, second = (
                delta[quad_of[member], part, half].astype(wide) for half in range(HALVES)
            )
            rows = [
                jnp.where(odd[member], second, first),
                jnp.where(odd[member], first, second),
            ]
            return jnp.concatenate(rows, axis=0).astype(half_type)

        fields = [
            [both_rows(member, part) for part in range(2)] for member in range(QUADS_STEP)
        ]

        def lift(image, part):
            member, channel = images[image]
            return bright(quad_of[member], channel) * fields[member][part]

        middle = dot(both_parts(lift), right_forward).astype(half_type)
        freq = dot(left_forward, to_rows(middle))

        def weigh(image, part):
            member, channel = images[image]
            factor = weight(quad_of[member], channel).astype(wide)
            return (piece(freq, image, part) * factor).astype(half_type)

        middle = dot(both_parts(weigh), right_inverse).astype(half_type)
        back = dot(left_inverse, to_rows(middle))
        for member, quad in enumerate(quad_of):
            for part in range(2):
                total = None
                for channel in range(channels):
                    term = bright(quad, channel).astype(wide) * piece(
                        back, images.index((member, channel)), part
                    )
                    total = term if total is None else total + term
                even_rows, odd_rows = total[:HALF_ROWS], total[HALF_ROWS:]
                chunks = (
                    jnp.where(odd[member], odd_rows, even_rows),
                    jnp.where(odd[member], even_rows, odd_rows),
                )
                for half in range(HALVES):
                    out[quad, part, half] = chunks[half].astype(half_type)
        return carry

    lax.fori_loop(0, (quads + QUADS_STEP - 1) // QUADS_STEP, visit, 0)


def product_kernel(
    channels_total,
    meta,
    kept,
    over_two,
    beams,
    turned,
    out_own,
    out_chips,
    out_sibling,
    totals_p0,
    totals_p1,
    totals_q0,
    totals_q1,
    turn,
):
    live = meta[5, 0]
    quads = (live + GROUP - 1) // GROUP
    totals_p, totals_q = (totals_p0, totals_p1), (totals_q0, totals_q1)
    for totals in totals_p + totals_q:
        totals[...] = jnp.zeros_like(totals)
    group = group_index(HALF_ROWS)
    scale = 1.0 / channels_total

    def add(quad, turn):
        for half in range(HALVES):
            for part in range(2):
                total = kept[quad, part, half].astype(jnp.float32)
                total = total + over_two[quad, part, half].astype(jnp.float32)
                total = total * scale
                for low in range(2):
                    turn[half, part, pl.ds(low, 8, stride=2), :] = total[low * 8 : (low + 1) * 8]
        for half in range(HALVES):
            real, imag = turn[half, 0], turn[half, 1]
            real_high, imag_high = swap_halves(real), swap_halves(imag)
            for member in range(GROUP):
                slot = quad * GROUP + member
                rows = pl.ds(meta[(2, 4)[half], slot], HALF_ROWS)
                station_p, station_q = meta[0, slot], meta[1, slot]
                shift = lax.rem(meta[3, slot] + 2 * G - member * W, 2 * G)
                alive = slot < live
                low = (group == member) & alive
                high = (group == (member + 2) % GROUP) & alive
                grad_real = jnp.where(low, real, jnp.where(high, real_high, 0.0))
                grad_imag = jnp.where(low, -imag, jnp.where(high, imag_high, 0.0))
                grad_real = pltpu.roll(grad_real, shift, 1)
                grad_imag = pltpu.roll(grad_imag, shift, 1)
                totals_p[half][station_p, rows, :] += (
                    beams[station_q, half, rows, :] * grad_real
                    + turned[station_q, half, rows, :] * grad_imag
                )
                totals_q[half][station_q, rows, :] += (
                    beams[station_p, half, rows, :] * grad_real
                    - turned[station_p, half, rows, :] * grad_imag
                )

    def visit(step, carry):
        for later in range(2):
            add(2 * step + later, turn.at[later])
        return carry

    lax.fori_loop(0, (quads + 1) // 2, visit, 0)

    def total(block, half):
        stations = pl.ds(block * ST_DEV, ST_DEV)
        return totals_p[half][stations] + totals_q[half][stations]

    for half in range(HALVES):
        out_own[:, half] = total(0, half)
        for block in range(2):
            out_chips[block, :, half] = total(1 + block, half)
            out_sibling[block, :, half] = total(3 + block, half).astype(jnp.bfloat16)


def result_kernel(mine, over_two, over_one, out, stage):
    chan = lax.axis_index("chan")
    high, low = chan % 2, chan // 2 % 2
    lower = lane_index(G // 2) < G
    for turn, value in enumerate((mine, over_two, over_one.at[0], over_one.at[1])):
        pol = (high ^ (turn // 2)) * 2 + (low ^ (turn % 2))
        for station in range(ST_DEV):
            even = value[station, 0].astype(jnp.float32)
            odd = value[station, 1].astype(jnp.float32)
            real = jnp.where(lower, even, swap_halves(odd))
            imag = jnp.where(lower, swap_halves(even), odd)
            stage[station, pl.ds(pol, G // 2, stride=2 * POLS), :] = real
            stage[station, pl.ds(pol + POLS, G // 2, stride=2 * POLS), :] = imag
    for station in range(ST_DEV):
        for pair in range(G // 2):
            out[station, :, pair * 2 * G : (pair + 1) * 2 * G] = stage[
                station, pair * 2 * POLS : (pair + 1) * 2 * POLS, :
            ]


def call(kernel, out_shape, in_specs, scratch_shapes, mebibytes=20):
    return pl.pallas_call(
        kernel,
        out_shape=out_shape,
        in_specs=in_specs,
        out_specs=jax.tree.map(lambda _: pl.BlockSpec(memory_space=VMEM), out_shape),
        scratch_shapes=scratch_shapes,
        compiler_params=pltpu.CompilerParams(vmem_limit_bytes=mebibytes * 1024 * 1024),
    )


def per_device(screens, direction, sky, weights, pairs, pointing, counts):
    base_count = lax.axis_size("base")
    myself = lax.axis_index("base")
    channels_total = CH_DEV * lax.axis_size("chan")
    core, chip_odd = myself % 2, myself // 2 % 2
    in_smem = pl.BlockSpec(memory_space=SMEM)
    in_vmem = pl.BlockSpec(memory_space=VMEM)

    both = jnp.concatenate([weights, sky])
    both, screens, direction = lax.optimization_barrier((both, screens, direction))
    own = call(
        own_kernel,
        jax.ShapeDtypeStruct((ST_DEV, 2, HALVES, G // 2, 2 * G), jnp.bfloat16),
        [in_vmem] * 2,
        [pltpu.VMEM((2 * ST_DEV, G * POLS, 2 * G), jnp.float32)],
    )(screens, direction)
    chip_a = across_chips(own, 0)
    meta = call(
        slots_kernel,
        jax.ShapeDtypeStruct((8, SUB_DEV), jnp.int32),
        [in_vmem] * 2 + [in_smem],
        [],
    )(pairs.T, pointing[None], counts)
    chip_b = across_chips(own, 1)
    both, meta = lax.optimization_barrier((both, meta))
    other = across_chan(both, 1)
    meta, chip_a, chip_b = lax.optimization_barrier((meta, chip_a, chip_b))
    shared_is_a = core == chip_odd
    sibling = to_sibling(jnp.stack([own, jnp.where(shared_is_a, chip_a, chip_b)]))

    delta_shape = (QUADS, 2, HALVES, HALF_ROWS, LANES)
    turn = pltpu.VMEM((HALVES, 2, HALF_ROWS, LANES), jnp.float32)
    field_shape = (NEAR * ST_DEV, HALVES, G // 2, 2 * G)
    field = pltpu.VMEM(field_shape, jnp.float32)
    delta, beams, turned = call(
        delta_kernel,
        [jax.ShapeDtypeStruct(delta_shape, jnp.bfloat16)]
        + [jax.ShapeDtypeStruct(field_shape, jnp.float32)] * 2,
        [in_smem] + [in_vmem] * 4,
        [field, pltpu.VMEM((2, HALVES, 2, HALF_ROWS, LANES), jnp.float32)],
    )(meta, own, chip_a, chip_b, sibling)
    over_two = across_chan(delta, 2)
    wide = jnp.float32
    tables = pass_tables()
    quad_shape = jax.ShapeDtypeStruct((QUADS, CH_DEV, W, LANES), jnp.bfloat16)

    mover = group_table()

    def prepared(weights, sky, first):
        return call(
            functools.partial(prepare_kernel, first),
            [quad_shape] * 2,
            [in_smem] + [in_vmem] * 3,
            [
                pltpu.VMEM((SUB_DEV, 8 * CH_DEV, LANES), wide),
                pltpu.VMEM((point_count, 8 * CH_DEV, LANES), wide),
            ],
        )(meta, weights, sky, mover)

    point_count = sky.shape[0]
    own_images = prepared(weights, sky, 0)
    other_images = prepared(other, other, SUB_DEV)
    weighting, brightness = zip(own_images, other_images)

    def hessian(delta):
        return call(
            hessian_kernel,
            jax.ShapeDtypeStruct(delta_shape, jnp.bfloat16),
            [in_smem] + [in_vmem] * 6,
            [],
            40,
        )(meta, delta, *weighting, *brightness, tables)

    sent, delta = lax.optimization_barrier((hessian(over_two), delta))
    back_two = across_chan(sent, 2)
    kept = hessian(delta)

    def make_product(*args):
        return product_kernel(channels_total, *args)

    block_shape = (ST_DEV, HALVES, G // 2, 2 * G)
    sum_own, sum_chips, sum_sibling = call(
        make_product,
        [
            jax.ShapeDtypeStruct(block_shape, wide),
            jax.ShapeDtypeStruct((2,) + block_shape, wide),
            jax.ShapeDtypeStruct((2,) + block_shape, jnp.bfloat16),
        ],
        [in_smem] + [in_vmem] * 4,
        [pltpu.VMEM((NEAR * ST_DEV, G // 2, 2 * G), wide)] * 4
        + [pltpu.VMEM((2, HALVES, 2, HALF_ROWS, LANES), wide)],
    )(meta, kept, back_two, beams, turned)
    from_sibling = to_sibling(sum_sibling).astype(wide)
    sum_a = sum_chips[0] + jnp.where(shared_is_a, from_sibling[1], 0.0)
    sum_b = sum_chips[1] + jnp.where(shared_is_a, 0.0, from_sibling[1])
    from_b = across_chips(sum_b.astype(jnp.bfloat16), 1)
    from_a = across_chips(sum_a.astype(jnp.bfloat16), 0)
    mine = sum_own + from_sibling[0] + from_b.astype(wide) + from_a.astype(wide)
    mine = mine.astype(jnp.bfloat16)
    other = across_chan(mine, 4)
    mine = (mine.astype(wide) + other.astype(wide)).astype(jnp.bfloat16)
    over_two = across_chan(mine, 2)
    over_one = across_chan(jnp.stack([mine, over_two]), 1)
    return call(
        result_kernel,
        jax.ShapeDtypeStruct((ST_DEV, 2 * POLS, G * G), wide),
        [in_vmem] * 3,
        [pltpu.VMEM((ST_DEV, G // 2 * 2 * POLS, 2 * G), wide)],
    )(mine, over_two, over_one)


def solution(mesh):
    in_specs = (
        P("base", None, None),
        P("base", None, None),
        P(None, "chan", None),
        P("base", "chan", None),
        P("base", None),
        P("base"),
        P("base"),
    )
    out_specs = P("base", None, None)
    return jax.shard_map(
        per_device, mesh=mesh, in_specs=in_specs, out_specs=out_specs, check_vma=False
    )
```
